512 devices in a mesh: dp: 16 (over x, y), expert: 32 (over z, core).
Axes of the slice: x: 4, y: 4, z: 16, core: 2. Of those that a mesh axis runs over, the one named last changes fastest.
Arguments:
- tokens: bfloat16 [65536, 1024], P(('dp', 'expert')), may hold values from -6 to 6
- expert_ids: int32 [65536, 6], P(('dp', 'expert')), may hold values from 0 to 63, all different within a row; in each aligned block of 128 rows (0 to 127, 128 to 255, ...) at most 13 rows name the same one
- router_gates: float32 [65536, 6], P(('dp', 'expert')), may hold values from 0.05 to 1
- w_in: bfloat16 [64, 2, 704, 1024], P('expert', None, 'dp'), may hold values from -0.1875 to 0.1875
- w_down: bfloat16 [64, 704, 1024], P('expert', 'dp'), may hold values from -0.21875 to 0.21875
- cotangent: bfloat16 [65536, 1024], P(('dp', 'expert')), may hold values from -6 to 6
Outputs:
- layer_output: bfloat16 [65536, 1024], P(('dp', 'expert'))
- token_grads: bfloat16 [65536, 1024], P(('dp', 'expert'))
- gate_grads: float32 [65536, 6], P(('dp', 'expert'))
The draws below stay inside these ranges and needn't reach their ends.
Inputs may be any that keep to these rules, and one draw needn't show every extreme that they name: `expert_ids`: each row names 6 different experts. The rows of one device name no expert more than 13 times, and in every draw some device names some expert exactly 13 times.
All inputs are finite; a program needn't handle non-finite values.
Results may differ from the reference program's by a relative error of at most 0.0064.
Values may be sent and summed in bfloat16 or wider, within the bound.
No kernel may reach another device: no remote copies, remote signals or barrier semaphores. Data moves between devices by JAX's collectives and lax.ppermute only.
A program may use at most 64 MiB of HBM per device.

```python
import math
import jax
import jax.numpy as jnp
import numpy as np
from jax import lax

D = 1024
FF = 704
TOPK = 6
TOK_DEV = 128
EXPERTS = 64
CAP = 13
TOKENS = 65536
DEVICES = 512


def level_of(rng, shape, shards, smallest, high):
    def one(axis_at, shards_of):
        heights = jax.random.uniform(jax.random.fold_in(jax.random.fold_in(rng, 6), axis_at), (shards_of,), jnp.float32, smallest / len(shards), high / len(shards))
        return jnp.repeat(jnp.exp(heights), shape[axis_at] // shards_of).reshape((-1,) + (1,) * (len(shape) - axis_at - 1))

    level = one(*shards[0])
    for cut in shards[1:]:
        level = level * one(*cut)
    return level


def shared_out(key, own, number, rows, count, top, most, slope):
    order = jax.random.permutation(key, count)
    packed, common = load_shares(count, rows * top, most, slope, True), load_shares(count, rows * top, most, slope, False)
    places = jnp.arange(count)

    def named(tallies, offset_by):
        used = int((tallies > 0).sum())
        fixed = max(1, used // 4)
        shifted = fixed + (places - fixed + offset_by * (used - fixed)) % max(1, count - fixed)
        return jnp.zeros((count,), jnp.int32).at[order[jnp.where(places < fixed, places, shifted)]].set(jnp.asarray(tallies, jnp.int32))

    tallies = jnp.where(number % 4 == 0, named(packed, number // 4), named(common, number - number // 4 - 1))
    mixed = jax.random.permutation(jax.random.fold_in(own, 3), count)
    giver, sink = mixed[0:count // 2 * 2:2], mixed[1:count // 2 * 2:2]
    margin = jnp.minimum(tallies[giver] - 1, most - tallies[sink]) // 2
    margin = jnp.where((giver == order[0]) | (sink == order[0]) | (tallies[sink] == 0), 0, jnp.maximum(margin, 0))
    shifted = jax.random.randint(jax.random.fold_in(own, 4), (count // 2,), 0, 1 << 20) % (margin + 1)
    tallies = tallies.at[giver].add(-shifted).at[sink].add(shifted)
    members = jnp.searchsorted(jnp.cumsum(tallies), jnp.arange(rows * top), side="right").astype(jnp.int32)
    grid = members.reshape(top, rows).T
    grid = grid[jax.random.permutation(jax.random.fold_in(own, 1), rows)]
    offset_by = jax.random.randint(jax.random.fold_in(own, 2), (rows, 1), 0, top)
    return jnp.take_along_axis(grid, (jnp.arange(top)[None, :] + offset_by) % top, axis=1)


def load_shares(number_of, total, most, lean, full):
    weights = [(1 << 20) // math.isqrt(standing ** lean) + 1 for standing in range(1, number_of + 1)]
    largest = most if full else min(most, max(-(-total // number_of), total * weights[0] // sum(weights)))
    least = 1 if total - largest >= number_of - 1 else 0
    given, spare = [largest] + [least] * (number_of - 1), total - largest - least * (number_of - 1)
    while spare > 0:
        free = [i for i in range(1, number_of) if given[i] < largest] or [i for i in range(1, number_of) if given[i] < most]
        whole, left = sum([weights[i] for i in free]), spare
        for i in free:
            extra = min(most - given[i], max(1, left * weights[i] // whole), spare)
            given[i] = given[i] + extra
            spare = spare - extra
    return np.array(given)


def gaussian(rng, dims, scale, most, pieces=(), kind=jnp.bfloat16):
    drawn = scale * jax.random.normal(rng, dims, jnp.float32)
    if pieces:
        drawn = drawn * level_of(rng, dims, pieces, -0.22, 0.18)
    return jnp.clip(drawn, -most, most).astype(kind)


def setup_inputs(seed: int = 0) -> dict:
    seeds = jax.random.split(jax.random.key(seed), 7)
    tokens = gaussian(seeds[0], (TOKENS, D), 1.0, 6.0, ((0, 512),))
    expert_ids_keys = jax.random.split(jax.random.fold_in(seeds[1], 1), TOKENS // TOK_DEV)
    expert_ids_turns = jax.random.permutation(jax.random.fold_in(seeds[1], 3), TOKENS // TOK_DEV)
    expert_ids = jax.vmap(lambda own, number: shared_out(jax.random.fold_in(seeds[1], 2), own, number, TOK_DEV, EXPERTS, TOPK, CAP, 1))(expert_ids_keys, expert_ids_turns).reshape((TOKENS, TOPK))
    router_gates = jnp.clip(jnp.exp(math.log(1.0) - 2.9957323 * jax.random.uniform(seeds[2], (TOKENS, TOPK), jnp.float32) ** level_of(seeds[2], (TOKENS, TOPK), ((0, 512),), -0.2, 0.2)), 0.05, 1.0)
    w_in = gaussian(seeds[3], (EXPERTS, 2, FF, D), D ** -0.5, 0.1875, ((0, 32), (2, 16)))
    w_down = gaussian(seeds[4], (EXPERTS, FF, D), FF ** -0.5, 0.21875, ((0, 32), (1, 16)))
    cotangent = gaussian(seeds[5], (TOKENS, D), 1.0, 6.0, ((0, 512),))
    return dict(tokens=tokens, expert_ids=expert_ids, router_gates=router_gates, w_in=w_in, w_down=w_down, cotangent=cotangent)


def expert_pass(rows_x, rows_grad, w_gate, w_up, w_out):
    gate_pre = jnp.dot(rows_x, w_gate.T, preferred_element_type=jnp.float32)
    up_pre = jnp.dot(rows_x, w_up.T, preferred_element_type=jnp.float32)
    sigmoid_gate = jax.nn.sigmoid(gate_pre)
    activated = gate_pre * sigmoid_gate
    hidden = (activated * up_pre).astype(jnp.bfloat16)
    expert_out = jnp.dot(hidden, w_out, preferred_element_type=jnp.float32).astype(jnp.bfloat16)
    grad_hidden = jnp.dot(rows_grad, w_out.T, preferred_element_type=jnp.float32)
    grad_up = (grad_hidden * activated).astype(jnp.bfloat16)
    grad_gate = (grad_hidden * up_pre * sigmoid_gate * (1.0 + gate_pre * (1.0 - sigmoid_gate))).astype(jnp.bfloat16)
    expert_grad = jnp.dot(grad_gate, w_gate, preferred_element_type=jnp.float32)
    expert_grad = expert_grad + jnp.dot(grad_up, w_up, preferred_element_type=jnp.float32)
    return expert_out, expert_grad.astype(jnp.bfloat16)


def reference(tokens, expert_ids, router_gates, w_in, w_down, cotangent):
    token_total = tokens.shape[0]
    assign_total = token_total * TOPK
    slot_span = DEVICES * CAP
    flat_ids = expert_ids.reshape(-1).astype(jnp.int32)
    flat_gates = router_gates.reshape(-1)
    sorted_slots = jnp.argsort(flat_ids, stable=True).astype(jnp.int32)
    counts = jnp.zeros((EXPERTS,), jnp.int32).at[flat_ids].add(1)
    offsets = (jnp.cumsum(counts) - counts).astype(jnp.int32)
    padded = jnp.concatenate([sorted_slots, jnp.full((slot_span,), assign_total, jnp.int32)])

    def step(carry, expert):
        out_acc, grad_acc, gate_acc = carry
        picked = lax.dynamic_slice_in_dim(padded, offsets[expert], slot_span)
        is_live = jnp.arange(slot_span, dtype=jnp.int32) < counts[expert]
        picked = jnp.where(is_live, picked, assign_total).astype(jnp.int32)
        token_index = jnp.where(is_live, picked // TOPK, 0).astype(jnp.int32)
        gate_value = jnp.where(is_live, flat_gates[jnp.minimum(picked, assign_total - 1)], jnp.zeros((), router_gates.dtype))
        rows_x = tokens[token_index]
        rows_cot = cotangent[token_index].astype(jnp.float32)
        rows_grad = (gate_value[:, None] * rows_cot).astype(jnp.bfloat16)
        weights = w_in[expert]
        expert_out, expert_grad = expert_pass(rows_x, rows_grad, weights[0], weights[1], w_down[expert])
        out_acc = out_acc.at[token_index].add(gate_value[:, None] * expert_out.astype(jnp.float32))
        grad_acc = grad_acc.at[token_index].add(jnp.where(is_live[:, None], expert_grad.astype(jnp.float32), 0.0))
        gate_acc = gate_acc.at[picked].set(jnp.sum(rows_cot * expert_out.astype(jnp.float32), axis=1))
        return (out_acc, grad_acc, gate_acc), None

    start = (jnp.zeros(tokens.shape, jnp.float32), jnp.zeros(tokens.shape, jnp.float32), jnp.zeros((assign_total + 1,), jnp.float32))
    final, unused = lax.scan(step, start, jnp.arange(EXPERTS, dtype=jnp.int32))
    out_acc, grad_acc, gate_acc = final
    layer_output = out_acc.astype(jnp.bfloat16)
    token_grads = grad_acc.astype(jnp.bfloat16)
    gate_grads = gate_acc[:assign_total].reshape(token_total, TOPK)
    return layer_output, token_grads, gate_grads
```

```python
import jax
import jax.numpy as jnp
from jax import lax
from jax.experimental import pallas as pl
from jax.experimental.pallas import tpu as pltpu
from jax.sharding import PartitionSpec as P

SLOTS = 16
VMEM = 56 * 1024 * 1024
NT = (((1,), (1,)), ((), ()))


def gather_kernel(rank_ref, rows_ref, x_ref, c_ref):
    tok = rank_ref.shape[2]
    model = rows_ref.shape[2]
    part = 8
    x = rows_ref[0, 0:tok, :]
    c = rows_ref[0, tok : 2 * tok, :]
    slot = lax.broadcasted_iota(jnp.int32, (part, SLOTS, tok), 1).astype(jnp.float32)

    def step(at, carry):
        first = pl.multiple_of(at * part, part)
        ranks = rank_ref[0, pl.ds(first, part), :]
        pick = jnp.where(ranks[:, None, :] == slot, 1.0, 0.0).astype(jnp.bfloat16)
        pick = pick.reshape(part * SLOTS, tok)
        xs = jnp.dot(pick, x, preferred_element_type=jnp.float32).astype(jnp.bfloat16)
        x_ref[pl.ds(first, part)] = xs.reshape(part, SLOTS, model)
        cs = jnp.dot(pick, c, preferred_element_type=jnp.float32).astype(jnp.bfloat16)
        c_ref[pl.ds(first, part)] = cs.reshape(part, SLOTS, model)
        return carry

    lax.fori_loop(0, x_ref.shape[0] // part, step, 0)


def combine(expert, group, rank_ref, slots_ref, total_ref, out_ref, rows):
    sources, tok = rank_ref.shape[0], rank_ref.shape[2]
    at = lax.rem(expert, group)
    model = rows.shape[1]
    slots_ref[:, pl.ds(pl.multiple_of(at * SLOTS, SLOTS), SLOTS), :] = rows.reshape(
        sources, SLOTS, model
    )
    slot = lax.broadcasted_iota(jnp.int32, (group, SLOTS, tok), 1).astype(jnp.float32)

    def sums(s, first):
        ranks = rank_ref[s, first : first + group, :]
        place = jnp.where(ranks[:, None, :] == slot, 1.0, 0.0).reshape(group * SLOTS, tok)
        place = jnp.transpose(place).astype(jnp.bfloat16)
        return jnp.dot(place, slots_ref[s], preferred_element_type=jnp.float32)

    @pl.when(expert == group - 1)
    def _():
        def one(s, carry):
            total_ref[s] = sums(s, 0)
            return carry

        lax.fori_loop(0, sources, one, 0)

    @pl.when(expert == 2 * group - 1)
    def _():
        def one(s, carry):
            out_ref[s] = (total_ref[s] + sums(s, group)).astype(out_ref.dtype)
            return carry

        lax.fori_loop(0, sources, one, 0)


def forward_kernel(w_ref, x_ref, c_ref, g_ref, rank_ref, out_ref, pair_ref, dot_ref, slots, total):
    expert = pl.program_id(0)
    hidden = w_ref.shape[1] // 3
    gate_up = w_ref[0, 0 : 2 * hidden, :]
    down = w_ref[0, 2 * hidden : 3 * hidden, :]
    pre = lax.dot_general(x_ref[0], gate_up, NT, preferred_element_type=jnp.float32)
    back = lax.dot_general(c_ref[0], down, NT, preferred_element_type=jnp.float32)
    gate = pre[:, 0:hidden]
    up = pre[:, hidden : 2 * hidden]
    sig = 1.0 / (1.0 + jnp.exp(-gate))
    act = gate * sig
    hid = act * up
    scale = jnp.transpose(g_ref[0])[:, 0:1]
    rows = jnp.dot(
        (hid * scale).astype(jnp.bfloat16), down, preferred_element_type=jnp.float32
    ).astype(jnp.bfloat16)
    prod = hid * back
    high = prod.astype(jnp.bfloat16)
    low = (prod - high.astype(jnp.float32)).astype(jnp.bfloat16)
    ones = jnp.ones((8, hidden), jnp.bfloat16)
    dot_ref[0] = lax.dot_general(ones, high, NT, preferred_element_type=jnp.float32) + (
        lax.dot_general(ones, low, NT, preferred_element_type=jnp.float32)
    )
    scaled = back * scale
    grad_up = scaled * act
    grad_gate = scaled * up * sig * (1.0 + gate * (1.0 - sig))
    pair_ref[0] = jnp.concatenate([grad_gate, grad_up], axis=1).astype(jnp.bfloat16)
    combine(expert, pl.num_programs(0) // 2, rank_ref, slots, total, out_ref, rows)


def backward_kernel(w_ref, pair_ref, rank_ref, out_ref, slots, total):
    expert = pl.program_id(0)
    rows = jnp.dot(pair_ref[0], w_ref[0], preferred_element_type=jnp.float32)
    combine(
        expert, pl.num_programs(0) // 2, rank_ref, slots, total, out_ref, rows.astype(jnp.bfloat16)
    )


def params():
    return pltpu.CompilerParams(dimension_semantics=("arbitrary",), vmem_limit_bytes=VMEM)


def gather_rows(ranks, rows):
    sources, half, tok = ranks.shape
    model = rows.shape[2]
    shape = jax.ShapeDtypeStruct((half, sources * SLOTS, model), jnp.bfloat16)
    block = pl.BlockSpec((half, SLOTS, model), lambda s: (0, s, 0))
    return pl.pallas_call(
        gather_kernel,
        grid=(sources,),
        in_specs=[
            pl.BlockSpec((1, half, tok), lambda s: (s, 0, 0)),
            pl.BlockSpec((1, rows.shape[1], model), lambda s: (s, 0, 0)),
        ],
        out_specs=[block, block],
        out_shape=[shape, shape],
        compiler_params=params(),
        cost_estimate=pl.CostEstimate(
            flops=4 * sources * half * SLOTS * tok * model,
            bytes_accessed=4 * half * sources * SLOTS * model + 2 * rows.size,
            transcendentals=0,
        ),
        name="gather_rows",
    )(ranks, rows)


def forward(weights, x_rows, c_rows, scales, ranks):
    half, w_rows, model = weights.shape
    hidden = w_rows // 3
    sources, _, tok = ranks.shape
    rows = sources * SLOTS
    each = lambda e: (e, 0, 0)
    whole = lambda e: (0, 0, 0)
    return pl.pallas_call(
        forward_kernel,
        grid=(half,),
        in_specs=[
            pl.BlockSpec((1, w_rows, model), each),
            pl.BlockSpec((1, rows, model), each),
            pl.BlockSpec((1, rows, model), each),
            pl.BlockSpec((1, 8, rows), each),
            pl.BlockSpec((sources, half, tok), whole),
        ],
        out_specs=[
            pl.BlockSpec((sources, tok, model), whole),
            pl.BlockSpec((1, rows, 2 * hidden), each),
            pl.BlockSpec((1, 8, rows), each),
        ],
        out_shape=[
            jax.ShapeDtypeStruct((sources, tok, model), jnp.bfloat16),
            jax.ShapeDtypeStruct((half, rows, 2 * hidden), jnp.bfloat16),
            jax.ShapeDtypeStruct((half, 8, rows), jnp.float32),
        ],
        scratch_shapes=[
            pltpu.VMEM((sources, half * SLOTS // 2, model), jnp.bfloat16),
            pltpu.VMEM((sources, tok, model), jnp.float32),
        ],
        compiler_params=params(),
        cost_estimate=pl.CostEstimate(
            flops=8 * half * rows * hidden * model,
            bytes_accessed=2 * (weights.size + x_rows.size + c_rows.size),
            transcendentals=half * rows * hidden,
        ),
        name="forward_experts",
    )(weights, x_rows, c_rows, scales, ranks)


def backward(weights, pairs, ranks):
    half, w_rows, model = weights.shape
    width = pairs.shape[2]
    sources, _, tok = ranks.shape
    rows = sources * SLOTS
    each = lambda e: (e, 0, 0)
    whole = lambda e: (0, 0, 0)
    return pl.pallas_call(
        backward_kernel,
        grid=(half,),
        in_specs=[
            pl.BlockSpec((1, width, model), each),
            pl.BlockSpec((1, rows, width), each),
            pl.BlockSpec((sources, half, tok), whole),
        ],
        out_specs=pl.BlockSpec((sources, tok, model), whole),
        out_shape=jax.ShapeDtypeStruct((sources, tok, model), jnp.bfloat16),
        scratch_shapes=[
            pltpu.VMEM((sources, half * SLOTS // 2, model), jnp.bfloat16),
            pltpu.VMEM((sources, tok, model), jnp.float32),
        ],
        compiler_params=params(),
        cost_estimate=pl.CostEstimate(
            flops=2 * half * rows * width * model,
            bytes_accessed=2 * (half * width * model + pairs.size),
            transcendentals=0,
        ),
        name="backward_experts",
    )(weights, pairs, ranks)


def body(tokens, expert_ids, router_gates, w_in, w_down, cotangent):
    tok, model = tokens.shape
    planes = lax.axis_size("dp")
    side = 4
    half = lax.axis_size("expert")
    experts = 2 * half
    parity = lax.rem(lax.axis_index("dp") // side, 2)

    def both_slices(which):
        pair = lax.dynamic_index_in_dim(w_in, which, 0, keepdims=False)
        down = lax.dynamic_slice_in_dim(w_down, which, 1, 0)
        return jnp.concatenate([pair, down], axis=0)

    swap = [(d, (((d // side) ^ 1) * side) + d % side) for d in range(planes)]
    other = lax.ppermute(both_slices(1 - parity), "dp", swap)
    mine = jnp.concatenate([both_slices(parity), other], axis=1).reshape(-1, model)
    weights = lax.all_gather(mine, "expert", axis=0, tiled=False)

    ids = expert_ids.T
    match = ids[:, None, :] == jnp.arange(experts, dtype=jnp.int32)[None, :, None]
    chosen = jnp.any(match, axis=0)
    gate_of = jnp.sum(jnp.where(match, router_gates.T[:, None, :], 0.0), axis=0)
    earlier = jnp.arange(tok)[:, None] < jnp.arange(tok)[None, :]
    rank = jnp.dot(
        chosen.astype(jnp.bfloat16), earlier.astype(jnp.bfloat16), preferred_element_type=jnp.float32
    )
    rank = jnp.where(chosen, rank, -1.0)
    slot_no = jnp.arange(SLOTS, dtype=jnp.float32)
    at_slot = rank[:, None, :] == slot_no[None, :, None]
    slot_gate = jnp.sum(jnp.where(at_slot, gate_of[:, None, :], 0.0), axis=2)
    gate_high = lax.reduce_precision(slot_gate, 8, 7)
    gate_low = slot_gate - gate_high

    def facts(odd):
        flat = lambda a: a.reshape(half, 2, -1)[:, odd].reshape(-1)
        return jnp.concatenate([flat(rank), flat(gate_high), flat(gate_low)]).astype(jnp.bfloat16)

    fact_rows = 16
    known = jnp.stack([facts(0), facts(1)])
    known = jnp.pad(known, ((0, 0), (0, fact_rows * model - known.shape[1])))
    known = known.reshape(2, 1, fact_rows, model)
    known = jnp.broadcast_to(known[:, None], (2, side, 1, fact_rows, model)).reshape(
        1, 2 * side, fact_rows, model
    )
    known = jnp.broadcast_to(known, (planes // (2 * side), 2 * side, fact_rows, model))
    known = known.reshape(planes, fact_rows, model)
    own = jnp.concatenate([tokens, cotangent], axis=0)
    sent = jnp.concatenate([jnp.broadcast_to(own[None], (planes, 2 * tok, model)), known], axis=1)
    rows = lax.all_to_all(sent, "dp", split_axis=0, concat_axis=0, tiled=True)

    facts_in = rows[:, 2 * tok :, :].reshape(planes, fact_rows * model).astype(jnp.float32)
    first, second = half * tok, half * tok + half * SLOTS
    ranks = facts_in[:, 0:first].reshape(planes, half, tok)
    scales = facts_in[:, first:second] + facts_in[:, second : second + half * SLOTS]
    scales = scales.reshape(planes, half, SLOTS).swapaxes(0, 1).reshape(half, 1, planes * SLOTS)
    scales = jnp.broadcast_to(scales, (half, 8, planes * SLOTS))

    x_rows, c_rows = gather_rows(ranks, rows)
    layer_part, pairs, dots = forward(weights, x_rows, c_rows, scales, ranks)
    layer_in = lax.all_to_all(layer_part, "dp", split_axis=0, concat_axis=0, tiled=True)
    grad_part = backward(weights, pairs, ranks)
    grad_in = lax.all_to_all(grad_part, "dp", split_axis=0, concat_axis=0, tiled=True)

    dots = dots[:, 0, :].reshape(half, planes, SLOTS).swapaxes(0, 1)
    even = jnp.where(parity == 0, dots, 0.0)
    odd = jnp.where(parity == 1, dots, 0.0)
    dots = jnp.stack([even, odd], axis=2).reshape(planes * 8, experts * SLOTS // 8)
    dots = lax.psum_scatter(dots, "dp", scatter_dimension=0, tiled=True)
    dots = dots.reshape(experts, SLOTS)
    by_expert = jnp.sum(jnp.where(at_slot, dots[:, :, None], 0.0), axis=1)
    gate_grads = jnp.sum(jnp.where(match, by_expert[None], 0.0), axis=1).T

    layer_output = jnp.sum(layer_in.astype(jnp.float32), axis=0).astype(jnp.bfloat16)
    token_grads = jnp.sum(grad_in.astype(jnp.float32), axis=0).astype(jnp.bfloat16)
    return (layer_output, token_grads, gate_grads)


def solution(mesh):
    both = P(("dp", "expert"), None)
    placed = (both, both, both, P("expert", None, "dp", None), P("expert", "dp", None), both)
    return jax.shard_map(
        body, mesh=mesh, in_specs=placed, out_specs=(both, both, both), check_vma=False
    )
```

```python
import jax
import jax.numpy as jnp
from jax import lax
from jax.experimental import pallas as pl
from jax.experimental.pallas import tpu as pltpu
from jax.sharding import PartitionSpec as P

STEP = 4
SLOTS = 16
VMEM = 56 * 1024 * 1024
NT = (((1,), (1,)), ((), ()))
TN = (((0,), (0,)), ((), ()))


def one_hot(ranks, slot):
    group, tok = ranks.shape
    hit = jnp.where(ranks[:, None, :] == slot, 1.0, 0.0)
    return hit.reshape(group * SLOTS, tok).astype(jnp.bfloat16)


def slot_numbers(group, tok):
    return lax.broadcasted_iota(jnp.int32, (group, SLOTS, tok), 1).astype(jnp.float32)


def gather_kernel(rank_ref, rows_ref, x_ref):
    half, tok = rank_ref.shape[1:]
    pick = one_hot(rank_ref[0], slot_numbers(half, tok))
    xs = jnp.dot(pick, rows_ref[0, 0:tok, :], preferred_element_type=jnp.float32)
    x_ref[...] = xs.astype(jnp.bfloat16).reshape(x_ref.shape)


def keep(expert, group, slots_ref, rows):
    at = lax.rem(expert, group)
    slots_ref[:, pl.ds(pl.multiple_of(at * SLOTS, SLOTS), SLOTS), :] = rows.reshape(
        slots_ref.shape[0], SLOTS, rows.shape[1]
    )


def combine(expert, group, rank_ref, slots_ref, total_ref, out_ref):
    sources, tok = rank_ref.shape[0], rank_ref.shape[2]
    slot = slot_numbers(group, tok)

    def sums(s, first):
        place = one_hot(rank_ref[s, first : first + group, :], slot)
        return lax.dot_general(place, slots_ref[s], TN, preferred_element_type=jnp.float32)

    @pl.when(expert == group - 1)
    def _():
        def one(s, carry):
            total_ref[s] = sums(s, 0)
            return carry

        lax.fori_loop(0, sources, one, 0)

    @pl.when(expert == 2 * group - 1)
    def _():
        def one(s, carry):
            out_ref[s, 0:tok, :] = (total_ref[s] + sums(s, group)).astype(out_ref.dtype)
            return carry

        lax.fori_loop(0, sources, one, 0)


def swish(pre, hidden):
    gate = pre[:, 0:hidden]
    up = pre[:, hidden : 2 * hidden]
    sig = 1.0 / (1.0 + jnp.exp(-gate))
    return gate, up, sig


def forward_kernel(w_ref, x_ref, g_ref, rank_ref, out_ref, pre_ref, slots, total):
    hidden = w_ref.shape[1] // 3
    group = STEP * pl.num_programs(0) // 2
    first = pl.program_id(0) * STEP
    for i in range(STEP):
        gate_up = w_ref[i, 0 : 2 * hidden, :]
        down = w_ref[i, 2 * hidden : 3 * hidden, :]
        pre = lax.dot_general(x_ref[i], gate_up, NT, preferred_element_type=jnp.float32)
        pre_ref[i] = pre
        gate, up, sig = swish(pre, hidden)
        scale = jnp.transpose(g_ref[i])[:, 0:1]
        scaled = (gate * sig * up * scale).astype(jnp.bfloat16)
        rows = jnp.dot(scaled, down, preferred_element_type=jnp.float32)
        keep(first + i, group, slots, rows.astype(jnp.bfloat16))
    combine(first + STEP - 1, group, rank_ref, slots, total, out_ref)


def backward_kernel(w_ref, pre_ref, g_ref, rank_ref, c_ref, out_ref, slots, total, dots):
    hidden = w_ref.shape[1] // 3
    half = STEP * pl.num_programs(0)
    group = half // 2
    first = pl.program_id(0) * STEP
    sources, tok, model = c_ref.shape

    @pl.when(lax.rem(first, group) == 0)
    def _():
        slot = slot_numbers(group, tok)

        def one(s, carry):
            ranks = rank_ref[s, pl.ds(pl.multiple_of(first, group), group), :]
            cs = jnp.dot(one_hot(ranks, slot), c_ref[s], preferred_element_type=jnp.float32)
            slots[s] = cs.astype(jnp.bfloat16)
            return carry

        lax.fori_loop(0, sources, one, 0)

    @pl.when(first == 0)
    def _():
        dots[...] = jnp.zeros_like(dots)

    lane = lax.broadcasted_iota(jnp.int32, dots.shape, 1)
    for i in range(STEP):
        gate_up = w_ref[i, 0 : 2 * hidden, :]
        down = w_ref[i, 2 * hidden : 3 * hidden, :]
        at = pl.multiple_of(lax.rem(first + i, group) * SLOTS, SLOTS)
        cs = slots[:, pl.ds(at, SLOTS), :].reshape(sources * SLOTS, model)
        back = lax.dot_general(cs, down, NT, preferred_element_type=jnp.float32)
        gate, up, sig = swish(pre_ref[i], hidden)
        act = gate * sig
        dot = jnp.sum(act * up * back, axis=1, keepdims=True)
        dots[...] = jnp.where(lane == first + i, dot, dots[...])
        scaled = back * jnp.transpose(g_ref[i])[:, 0:1]
        grad_up = scaled * act
        grad_gate = scaled * up * sig * (1.0 + gate * (1.0 - sig))
        pair = jnp.concatenate([grad_gate, grad_up], axis=1).astype(jnp.bfloat16)
        rows = jnp.dot(pair, gate_up, preferred_element_type=jnp.float32)
        keep(first + i, group, slots, rows.astype(jnp.bfloat16))
    combine(first + STEP - 1, group, rank_ref, slots, total, out_ref)

    @pl.when(first + STEP == half)
    def _():
        low_rows = SLOTS // 2

        def one(s, carry):
            part = dots[pl.ds(pl.multiple_of(s * SLOTS, SLOTS), SLOTS), 0:half]
            high = part.astype(jnp.bfloat16).astype(jnp.float32)
            low = part - high
            blank = jnp.zeros((low_rows, model - 4 * half), jnp.float32)
            line = [high[0:low_rows], low[0:low_rows], high[low_rows:], low[low_rows:], blank]
            out_ref[s, tok : tok + low_rows, :] = jnp.concatenate(line, axis=1).astype(jnp.bfloat16)
            return carry

        lax.fori_loop(0, sources, one, 0)


def params():
    return pltpu.CompilerParams(dimension_semantics=("arbitrary",), vmem_limit_bytes=VMEM)


def each(e):
    return (e, 0, 0)


def whole(e):
    return (0, 0, 0)


def gather_rows(ranks, rows):
    sources, half, tok = ranks.shape
    model = rows.shape[2]
    return pl.pallas_call(
        gather_kernel,
        grid=(sources,),
        in_specs=[
            pl.BlockSpec((1, half, tok), each),
            pl.BlockSpec((1, rows.shape[1], model), each),
        ],
        out_specs=pl.BlockSpec((half, SLOTS, model), lambda s: (0, s, 0)),
        out_shape=jax.ShapeDtypeStruct((half, sources * SLOTS, model), jnp.bfloat16),
        compiler_params=params(),
        cost_estimate=pl.CostEstimate(
            flops=2 * sources * half * SLOTS * tok * model,
            bytes_accessed=2 * half * sources * SLOTS * model + 2 * rows.size,
            transcendentals=0,
        ),
        name="gather_rows",
    )(ranks, rows)


def forward(weights, x_rows, scales, ranks):
    half, w_rows, model = weights.shape
    hidden = w_rows // 3
    sources, _, tok = ranks.shape
    rows = sources * SLOTS
    return pl.pallas_call(
        forward_kernel,
        grid=(half // STEP,),
        in_specs=[
            pl.BlockSpec((STEP, w_rows, model), each),
            pl.BlockSpec((STEP, rows, model), each),
            pl.BlockSpec((STEP, 8, rows), each),
            pl.BlockSpec((sources, half, tok), whole),
        ],
        out_specs=[
            pl.BlockSpec((sources, tok, model), whole),
            pl.BlockSpec((STEP, rows, 2 * hidden), each),
        ],
        out_shape=[
            jax.ShapeDtypeStruct((sources, tok, model), jnp.bfloat16),
            jax.ShapeDtypeStruct((half, rows, 2 * hidden), jnp.float32),
        ],
        scratch_shapes=[
            pltpu.VMEM((sources, half * SLOTS // 2, model), jnp.bfloat16),
            pltpu.VMEM((sources, tok, model), jnp.float32),
        ],
        compiler_params=params(),
        cost_estimate=pl.CostEstimate(
            flops=6 * half * rows * hidden * model,
            bytes_accessed=2 * (weights.size + x_rows.size),
            transcendentals=half * rows * hidden,
        ),
        name="forward_experts",
    )(weights, x_rows, scales, ranks)


def backward(weights, pre, scales, ranks, cotangents):
    half, w_rows, model = weights.shape
    sources, _, tok = ranks.shape
    rows = sources * SLOTS
    out_rows = tok + SLOTS // 2
    return pl.pallas_call(
        backward_kernel,
        grid=(half // STEP,),
        in_specs=[
            pl.BlockSpec((STEP, w_rows, model), each),
            pl.BlockSpec((STEP, rows, pre.shape[2]), each),
            pl.BlockSpec((STEP, 8, rows), each),
            pl.BlockSpec((sources, half, tok), whole),
            pl.BlockSpec((sources, tok, model), whole),
        ],
        out_specs=pl.BlockSpec((sources, out_rows, model), whole),
        out_shape=jax.ShapeDtypeStruct((sources, out_rows, model), jnp.bfloat16),
        scratch_shapes=[
            pltpu.VMEM((sources, half * SLOTS // 2, model), jnp.bfloat16),
            pltpu.VMEM((sources, tok, model), jnp.float32),
            pltpu.VMEM((rows, 128), jnp.float32),
        ],
        compiler_params=params(),
        cost_estimate=pl.CostEstimate(
            flops=6 * half * rows * (w_rows // 3) * model,
            bytes_accessed=2 * (weights.size + 2 * pre.size),
            transcendentals=half * rows * (w_rows // 3),
        ),
        name="backward_experts",
    )(weights, pre, scales, ranks, cotangents)


def body(tokens, expert_ids, router_gates, w_in, w_down, cotangent):
    tok, model = tokens.shape
    planes = lax.axis_size("dp")
    side = 4
    half = lax.axis_size("expert")
    experts = 2 * half
    parity = lax.rem(lax.axis_index("dp") // side, 2)

    def both_slices(which):
        pair = lax.dynamic_index_in_dim(w_in, which, 0, keepdims=False)
        down = lax.dynamic_slice_in_dim(w_down, which, 1, 0)
        return jnp.concatenate([pair, down], axis=0)

    swap = [(d, (((d // side) ^ 1) * side) + d % side) for d in range(planes)]
    other = lax.ppermute(both_slices(1 - parity), "dp", swap)
    mine = jnp.concatenate([both_slices(parity), other], axis=1).reshape(-1, model)
    weights = lax.all_gather(mine, "expert", axis=0, tiled=False)

    ids = expert_ids.T
    match = ids[:, None, :] == jnp.arange(experts, dtype=jnp.int32)[None, :, None]
    chosen = jnp.any(match, axis=0)
    gate_of = jnp.sum(jnp.where(match, router_gates.T[:, None, :], 0.0), axis=0)
    earlier = jnp.arange(tok)[:, None] < jnp.arange(tok)[None, :]
    rank = jnp.dot(
        chosen.astype(jnp.bfloat16), earlier.astype(jnp.bfloat16), preferred_element_type=jnp.float32
    )
    rank = jnp.where(chosen, rank, -1.0)
    slot_no = jnp.arange(SLOTS, dtype=jnp.float32)
    at_slot = rank[:, None, :] == slot_no[None, :, None]
    slot_gate = jnp.sum(jnp.where(at_slot, gate_of[:, None, :], 0.0), axis=2)
    gate_high = lax.reduce_precision(slot_gate, 8, 7)
    gate_low = slot_gate - gate_high

    def facts(odd):
        flat = lambda a: a.reshape(half, 2, -1)[:, odd].reshape(-1)
        return jnp.concatenate([flat(rank), flat(gate_high), flat(gate_low)]).astype(jnp.bfloat16)

    fact_rows = 8
    known = jnp.stack([facts(0), facts(1)])
    known = jnp.pad(known, ((0, 0), (0, fact_rows * model - known.shape[1])))
    known = known.reshape(2, 1, fact_rows, model)
    known = jnp.broadcast_to(known[:, None], (2, side, 1, fact_rows, model)).reshape(
        1, 2 * side, fact_rows, model
    )
    known = jnp.broadcast_to(known, (planes // (2 * side), 2 * side, fact_rows, model))
    known = known.reshape(planes, fact_rows, model)
    spread = lambda a: jnp.broadcast_to(a[None], (planes, tok, model))
    swap_rows = lambda a: lax.all_to_all(a, "dp", split_axis=0, concat_axis=0, tiled=True)
    rows = swap_rows(jnp.concatenate([spread(tokens), known], axis=1))
    cotangents = swap_rows(spread(cotangent))

    facts_in = rows[:, tok:, :].reshape(planes, fact_rows * model).astype(jnp.float32)
    first, second = half * tok, half * tok + half * SLOTS
    ranks = facts_in[:, 0:first].reshape(planes, half, tok)
    scales = facts_in[:, first:second] + facts_in[:, second : second + half * SLOTS]
    scales = scales.reshape(planes, half, SLOTS).swapaxes(0, 1).reshape(half, 1, planes * SLOTS)
    scales = jnp.broadcast_to(scales, (half, 8, planes * SLOTS))

    x_rows = gather_rows(ranks, rows)
    layer_part, pre = forward(weights, x_rows, scales, ranks)
    layer_output = lax.psum_scatter(
        layer_part.reshape(planes * tok, model), "dp", scatter_dimension=0, tiled=True
    )
    grad_in = swap_rows(backward(weights, pre, scales, ranks, cotangents)).astype(jnp.float32)
    token_grads = jnp.sum(grad_in[:, 0:tok], axis=0).astype(jnp.bfloat16)

    dots = grad_in[:, tok:, 0 : 4 * half].reshape(2, 2, side, SLOTS // 2, 2, 2, half)
    dots = jnp.sum(dots, axis=(0, 2, 5))
    dots = dots.transpose(3, 0, 2, 1).reshape(experts, SLOTS)
    by_expert = jnp.sum(jnp.where(at_slot, dots[:, :, None], 0.0), axis=1)
    gate_grads = jnp.sum(jnp.where(match, by_expert[None], 0.0), axis=1).T
    return (layer_output, token_grads, gate_grads)


def solution(mesh):
    both = P(("dp", "expert"), None)
    placed = (both, both, both, P("expert", None, "dp", None), P("expert", "dp", None), both)
    return jax.shard_map(
        body, mesh=mesh, in_specs=placed, out_specs=(both, both, both), check_vma=False
    )
```

```python
import jax
import jax.numpy as jnp
from jax import lax
from jax.experimental import pallas as pl
from jax.experimental.pallas import tpu as pltpu
from jax.sharding import PartitionSpec as P

STEP = 8
SLOTS = 16
VMEM = 56 * 1024 * 1024
NT = (((1,), (1,)), ((), ()))
TN = (((0,), (0,)), ((), ()))


def one_hot(ranks, slot):
    group, tok = ranks.shape
    hit = jnp.where(ranks[:, None, :] == slot, 1.0, 0.0)
    return hit.reshape(group * SLOTS, tok).astype(jnp.bfloat16)


def slot_numbers(group, tok):
    return lax.broadcasted_iota(jnp.int32, (group, SLOTS, tok), 1).astype(jnp.float32)


def gather_kernel(rank_ref, rows_ref, x_ref):
    half, tok = rank_ref.shape[1:]
    pick = one_hot(rank_ref[0], slot_numbers(half, tok))
    xs = jnp.dot(pick, rows_ref[0, 0:tok, :], preferred_element_type=jnp.float32)
    x_ref[...] = xs.astype(jnp.bfloat16).reshape(x_ref.shape)


def keep(expert, slots_ref, rows):
    at = pl.multiple_of(expert * SLOTS, SLOTS)
    slots_ref[:, pl.ds(at, SLOTS), :] = rows.reshape(slots_ref.shape[0], SLOTS, rows.shape[1])


def combine(rank_ref, slots_ref, *out_refs):
    sources, half, tok = rank_ref.shape
    slot = slot_numbers(half, tok)

    def one(s, carry):
        place = one_hot(rank_ref[s], slot)
        sums = lax.dot_general(place, slots_ref[s], TN, preferred_element_type=jnp.float32)
        start = 0
        for out_ref in out_refs:
            stop = start + out_ref.shape[2]
            out_ref[s, 0:tok, :] = sums[:, start:stop].astype(out_ref.dtype)
            start = stop
        return carry

    lax.fori_loop(0, sources, one, 0)


def swish(pre, hidden):
    gate = pre[:, 0:hidden]
    up = pre[:, hidden : 2 * hidden]
    sig = 1.0 / (1.0 + jnp.exp(-gate))
    return gate, up, sig


def forward_kernel(w_ref, x_ref, g_ref, rank_ref, out_ref, pre_ref, slots):
    hidden = w_ref.shape[1] // 3
    first = pl.program_id(0) * STEP
    kept = []
    for i in range(STEP):
        gate_up = w_ref[i, 0 : 2 * hidden, :]
        pre = lax.dot_general(x_ref[i], gate_up, NT, preferred_element_type=jnp.float32)
        pre_ref[i] = pre
        gate, up, sig = swish(pre, hidden)
        kept.append((gate * sig * up).astype(jnp.bfloat16))
    for i in range(STEP):
        down = w_ref[i, 2 * hidden : 3 * hidden, :]
        rows = jnp.dot(kept[i], down, preferred_element_type=jnp.float32)
        scale = jnp.transpose(g_ref[i])[:, 0:1]
        keep(first + i, slots, (rows * scale).astype(jnp.bfloat16))

    @pl.when(first + STEP == rank_ref.shape[1])
    def _():
        combine(rank_ref, slots, out_ref)


def backward_kernel(
    w_ref, pre_ref, g_ref, rank_ref, c_ref, out_ref, more_ref, slots, dots
):
    hidden = w_ref.shape[1] // 3
    first = pl.program_id(0) * STEP
    sources, tok, model = c_ref.shape
    half = rank_ref.shape[1]

    @pl.when(first == 0)
    def _():
        slot = slot_numbers(half, tok)

        def one(s, carry):
            cs = jnp.dot(one_hot(rank_ref[s], slot), c_ref[s], preferred_element_type=jnp.float32)
            scale = jnp.transpose(g_ref[s])[:, 0:1]
            slots[s] = (cs * scale).astype(jnp.bfloat16)
            return carry

        lax.fori_loop(0, sources, one, 0)
        dots[...] = jnp.zeros_like(dots)

    kept = []
    lane = lax.broadcasted_iota(jnp.int32, dots.shape, 1)
    found = dots[...]
    for i in range(STEP):
        down = w_ref[i, 2 * hidden : 3 * hidden, :]
        at = pl.multiple_of((first + i) * SLOTS, SLOTS)
        cs = slots[:, pl.ds(at, SLOTS), :].reshape(sources * SLOTS, model)
        back = lax.dot_general(cs, down, NT, preferred_element_type=jnp.float32)
        gate, up, sig = swish(pre_ref[i], hidden)
        act = gate * sig
        dot = jnp.sum(act * up * back, axis=1, keepdims=True)
        found = jnp.where(lane == first + i, dot, found)
        grad_up = back * act
        grad_gate = back * up * sig * (1.0 + gate * (1.0 - sig))
        kept.append(jnp.concatenate([grad_gate, grad_up], axis=1).astype(jnp.bfloat16))
    dots[...] = found
    for i in range(STEP):
        gate_up = w_ref[i, 0 : 2 * hidden, :]
        rows = jnp.dot(kept[i], gate_up, preferred_element_type=jnp.float32)
        keep(first + i, slots, rows.astype(jnp.bfloat16))

    @pl.when(first + STEP == half)
    def _():
        combine(rank_ref, slots, out_ref, more_ref)
        low_rows = SLOTS // 2

        def one(s, carry):
            part = dots[pl.ds(pl.multiple_of(s * SLOTS, SLOTS), SLOTS), 0:half]
            high = part.astype(jnp.bfloat16).astype(jnp.float32)
            low = part - high
            blank = jnp.zeros((low_rows, out_ref.shape[2] - 4 * half), jnp.float32)
            line = [high[0:low_rows], low[0:low_rows], high[low_rows:], low[low_rows:], blank]
            out_ref[s, tok : tok + low_rows, :] = jnp.concatenate(line, axis=1).astype(jnp.bfloat16)
            return carry

        lax.fori_loop(0, sources, one, 0)


def params():
    return pltpu.CompilerParams(dimension_semantics=("arbitrary",), vmem_limit_bytes=VMEM)


def each(e):
    return (e, 0, 0)


def whole(e):
    return (0, 0, 0)


def gather_rows(ranks, rows):
    sources, half, tok = ranks.shape
    model = rows.shape[2]
    return pl.pallas_call(
        gather_kernel,
        grid=(sources,),
        in_specs=[
            pl.BlockSpec((1, half, tok), each),
            pl.BlockSpec((1, rows.shape[1], model), each),
        ],
        out_specs=pl.BlockSpec((half, SLOTS, model), lambda s: (0, s, 0)),
        out_shape=jax.ShapeDtypeStruct((half, sources * SLOTS, model), jnp.bfloat16),
        compiler_params=params(),
        cost_estimate=pl.CostEstimate(
            flops=2 * sources * half * SLOTS * tok * model,
            bytes_accessed=2 * half * sources * SLOTS * model + 2 * rows.size,
            transcendentals=0,
        ),
        name="gather_rows",
    )(ranks, rows)


def forward(weights, x_rows, scales, ranks):
    half, w_rows, model = weights.shape
    hidden = w_rows // 3
    sources, _, tok = ranks.shape
    rows = sources * SLOTS
    return pl.pallas_call(
        forward_kernel,
        grid=(half // STEP,),
        in_specs=[
            pl.BlockSpec((STEP, w_rows, model), each),
            pl.BlockSpec((STEP, rows, model), each),
            pl.BlockSpec((STEP, 8, rows), each),
            pl.BlockSpec((sources, half, tok), whole),
        ],
        out_specs=[
            pl.BlockSpec((sources, tok, model), whole),
            pl.BlockSpec((STEP, rows, 2 * hidden), each),
        ],
        out_shape=[
            jax.ShapeDtypeStruct((sources, tok, model), jnp.bfloat16),
            jax.ShapeDtypeStruct((half, rows, 2 * hidden), jnp.float32),
        ],
        scratch_shapes=[
            pltpu.VMEM((sources, half * SLOTS, model), jnp.bfloat16),
        ],
        compiler_params=params(),
        cost_estimate=pl.CostEstimate(
            flops=6 * half * rows * hidden * model,
            bytes_accessed=2 * (weights.size + x_rows.size),
            transcendentals=half * rows * hidden,
        ),
        name="forward_experts",
    )(weights, x_rows, scales, ranks)


def backward(weights, pre, scales, ranks, cotangents):
    half, w_rows, model = weights.shape
    sources, _, tok = ranks.shape
    rows = sources * SLOTS
    out_rows = tok + SLOTS // 2
    return pl.pallas_call(
        backward_kernel,
        grid=(half // STEP,),
        in_specs=[
            pl.BlockSpec((STEP, w_rows, model), each),
            pl.BlockSpec((STEP, rows, pre.shape[2]), each),
            pl.BlockSpec((sources, 8, half * SLOTS), whole),
            pl.BlockSpec((sources, half, tok), whole),
            pl.BlockSpec((sources, tok, model), whole),
        ],
        out_specs=[
            pl.BlockSpec((sources, out_rows, model // 2), whole),
            pl.BlockSpec((sources, tok, model // 2), whole),
        ],
        out_shape=[
            jax.ShapeDtypeStruct((sources, out_rows, model // 2), jnp.bfloat16),
            jax.ShapeDtypeStruct((sources, tok, model // 2), jnp.bfloat16),
        ],
        scratch_shapes=[
            pltpu.VMEM((sources, half * SLOTS, model), jnp.bfloat16),
            pltpu.VMEM((rows, 128), jnp.float32),
        ],
        compiler_params=params(),
        cost_estimate=pl.CostEstimate(
            flops=6 * half * rows * (w_rows // 3) * model,
            bytes_accessed=2 * (weights.size + 2 * pre.size),
            transcendentals=half * rows * (w_rows // 3),
        ),
        name="backward_experts",
    )(weights, pre, scales, ranks, cotangents)


def body(tokens, expert_ids, router_gates, w_in, w_down, cotangent):
    tok, model = tokens.shape
    planes = lax.axis_size("dp")
    side = 4
    half = lax.axis_size("expert")
    experts = 2 * half
    parity = lax.rem(lax.axis_index("dp") // side, 2)

    def both_slices(which):
        pair = lax.dynamic_index_in_dim(w_in, which, 0, keepdims=False)
        down = lax.dynamic_slice_in_dim(w_down, which, 1, 0)
        return jnp.concatenate([pair, down], axis=0)

    swap = [(d, (((d // side) ^ 1) * side) + d % side) for d in range(planes)]
    other = lax.ppermute(both_slices(1 - parity), "dp", swap)
    mine = jnp.concatenate([both_slices(parity), other], axis=1).reshape(-1, model)
    weights = lax.all_gather(mine, "expert", axis=0, tiled=False)

    ids = expert_ids.T
    match = ids[:, None, :] == jnp.arange(experts, dtype=jnp.int32)[None, :, None]
    chosen = jnp.any(match, axis=0)
    gate_of = jnp.sum(jnp.where(match, router_gates.T[:, None, :], 0.0), axis=0)
    earlier = jnp.arange(tok)[:, None] < jnp.arange(tok)[None, :]
    rank = jnp.dot(
        chosen.astype(jnp.bfloat16), earlier.astype(jnp.bfloat16), preferred_element_type=jnp.float32
    )
    rank = jnp.where(chosen, rank, -1.0)
    slot_no = jnp.arange(SLOTS, dtype=jnp.float32)
    at_slot = rank[:, None, :] == slot_no[None, :, None]
    slot_gate = jnp.sum(jnp.where(at_slot, gate_of[:, None, :], 0.0), axis=2)
    gate_high = lax.reduce_precision(slot_gate, 8, 7)
    gate_low = slot_gate - gate_high

    def facts(odd):
        flat = lambda a: a.reshape(half, 2, -1)[:, odd].reshape(-1)
        return jnp.concatenate([flat(rank), flat(gate_high), flat(gate_low)]).astype(jnp.bfloat16)

    fact_rows = 8
    known = jnp.stack([facts(0), facts(1)])
    known = jnp.pad(known, ((0, 0), (0, fact_rows * model - known.shape[1])))
    known = known.reshape(2, 1, fact_rows, model)
    known = jnp.broadcast_to(known[:, None], (2, side, 1, fact_rows, model)).reshape(
        1, 2 * side, fact_rows, model
    )
    known = jnp.broadcast_to(known, (planes // (2 * side), 2 * side, fact_rows, model))
    known = known.reshape(planes, fact_rows, model)
    spread = lambda a: jnp.broadcast_to(a[None], (planes, tok, model))
    swap_rows = lambda a: lax.all_to_all(a, "dp", split_axis=0, concat_axis=0, tiled=True)
    rows = swap_rows(jnp.concatenate([spread(tokens), known], axis=1))
    cotangents = swap_rows(spread(cotangent))

    facts_in = rows[:, tok:, :].reshape(planes, fact_rows * model).astype(jnp.float32)
    first, second = half * tok, half * tok + half * SLOTS
    ranks = facts_in[:, 0:first].reshape(planes, half, tok)
    scales = facts_in[:, first:second] + facts_in[:, second : second + half * SLOTS]
    by_source = jnp.broadcast_to(scales[:, None], (planes, 8, half * SLOTS))
    scales = scales.reshape(planes, half, SLOTS).swapaxes(0, 1).reshape(half, 1, planes * SLOTS)
    scales = jnp.broadcast_to(scales, (half, 8, planes * SLOTS))

    scales = scales + 0.0 * cotangents[0, 0, 0].astype(jnp.float32)
    x_rows = gather_rows(ranks, rows)
    layer_part, pre = forward(weights, x_rows, scales, ranks)
    along_x = [[x * side + y for x in range(planes // side)] for y in range(side)]
    along_y = [[x * side + y for y in range(side)] for x in range(planes // side)]
    layer_x = lax.psum_scatter(
        layer_part.reshape(planes * tok, model),
        "dp",
        scatter_dimension=0,
        axis_index_groups=along_x,
        tiled=True,
    )
    first_part, second_part = backward(weights, pre, by_source, ranks, cotangents)
    first_in = swap_rows(first_part)
    layer_output = lax.psum_scatter(
        layer_x + 0.0 * first_in[0, 0, 0].astype(layer_x.dtype),
        "dp",
        scatter_dimension=0,
        axis_index_groups=along_y,
        tiled=True,
    )
    second_in = swap_rows(second_part).astype(jnp.float32)
    first_in = first_in.astype(jnp.float32)
    token_grads = jnp.concatenate(
        [jnp.sum(first_in[:, 0:tok], axis=0), jnp.sum(second_in, axis=0)], axis=1
    ).astype(jnp.bfloat16)

    dots = first_in[:, tok:, 0 : 4 * half].reshape(2, 2, side, SLOTS // 2, 2, 2, half)
    dots = jnp.sum(dots, axis=(0, 2, 5))
    dots = dots.transpose(3, 0, 2, 1).reshape(experts, SLOTS)
    by_expert = jnp.sum(jnp.where(at_slot, dots[:, :, None], 0.0), axis=1)
    gate_grads = jnp.sum(jnp.where(match, by_expert[None], 0.0), axis=1).T / router_gates
    return (layer_output, token_grads, gate_grads)


def solution(mesh):
    both = P(("dp", "expert"), None)
    placed = (both, both, both, P("expert", None, "dp", None), P("expert", "dp", None), both)
    return jax.shard_map(
        body, mesh=mesh, in_specs=placed, out_specs=(both, both, both), check_vma=False
    )
```

```python
import jax
import jax.numpy as jnp
from jax import lax
from jax.experimental import pallas as pl
from jax.experimental.pallas import tpu as pltpu
from jax.sharding import PartitionSpec as P

STEP = 8
SLOTS = 16
VMEM = 56 * 1024 * 1024
NT = (((1,), (1,)), ((), ()))
TN = (((0,), (0,)), ((), ()))


def one_hot(ranks, slot):
    group, tok = ranks.shape
    hit = jnp.where(ranks[:, None, :] == slot, 1.0, 0.0)
    return hit.reshape(group * SLOTS, tok).astype(jnp.bfloat16)


def slot_numbers(group, tok):
    return lax.broadcasted_iota(jnp.int32, (group, SLOTS, tok), 1).astype(jnp.float32)


def gather_kernel(rank_ref, rows_ref, x_ref):
    half, tok = rank_ref.shape[1:]
    pick = one_hot(rank_ref[0], slot_numbers(half, tok))
    xs = jnp.dot(pick, rows_ref[0, 0:tok, :], preferred_element_type=jnp.float32)
    x_ref[...] = xs.astype(jnp.bfloat16).reshape(x_ref.shape)


def keep(expert, slots_ref, rows):
    at = pl.multiple_of(expert * SLOTS, SLOTS)
    slots_ref[:, pl.ds(at, SLOTS), :] = rows.reshape(slots_ref.shape[0], SLOTS, rows.shape[1])


def combine(rank_ref, slots_ref, out_ref):
    sources, half, tok = rank_ref.shape
    slot = slot_numbers(half, tok)

    def one(s, carry):
        place = one_hot(rank_ref[s], slot)
        sums = lax.dot_general(place, slots_ref[s], TN, preferred_element_type=jnp.float32)
        out_ref[s, 0:tok, :] = sums.astype(out_ref.dtype)
        return carry

    lax.fori_loop(0, sources, one, 0)


def swish(pre, hidden):
    gate = pre[:, 0:hidden]
    up = pre[:, hidden : 2 * hidden]
    sig = 1.0 / (1.0 + jnp.exp(-gate))
    return gate, up, sig


def forward_kernel(w_ref, x_ref, g_ref, rank_ref, out_ref, pre_ref, slots):
    hidden = w_ref.shape[1] // 3
    first = pl.program_id(0) * STEP
    kept = []
    for i in range(STEP):
        gate_up = w_ref[i, 0 : 2 * hidden, :]
        pre = lax.dot_general(x_ref[i], gate_up, NT, preferred_element_type=jnp.float32)
        pre_ref[i] = pre
        gate, up, sig = swish(pre, hidden)
        kept.append((gate * sig * up).astype(jnp.bfloat16))
    for i in range(STEP):
        down = w_ref[i, 2 * hidden : 3 * hidden, :]
        rows = jnp.dot(kept[i], down, preferred_element_type=jnp.float32)
        scale = jnp.transpose(g_ref[i])[:, 0:1]
        keep(first + i, slots, (rows * scale).astype(jnp.bfloat16))

    @pl.when(first + STEP == rank_ref.shape[1])
    def _():
        combine(rank_ref, slots, out_ref)


def backward_kernel(w_ref, pre_ref, g_ref, rank_ref, c_ref, out_ref, slots, dots):
    hidden = w_ref.shape[1] // 3
    first = pl.program_id(0) * STEP
    sources, tok, model = c_ref.shape
    half = rank_ref.shape[1]

    @pl.when(first == 0)
    def _():
        slot = slot_numbers(half, tok)

        def one(s, carry):
            cs = jnp.dot(one_hot(rank_ref[s], slot), c_ref[s], preferred_element_type=jnp.float32)
            scale = jnp.transpose(g_ref[s])[:, 0:1]
            slots[s] = (cs * scale).astype(jnp.bfloat16)
            return carry

        lax.fori_loop(0, sources, one, 0)
        dots[...] = jnp.zeros_like(dots)

    kept = []
    lane = lax.broadcasted_iota(jnp.int32, dots.shape, 1)
    found = dots[...]
    for i in range(STEP):
        down = w_ref[i, 2 * hidden : 3 * hidden, :]
        at = pl.multiple_of((first + i) * SLOTS, SLOTS)
        cs = slots[:, pl.ds(at, SLOTS), :].reshape(sources * SLOTS, model)
        back = lax.dot_general(cs, down, NT, preferred_element_type=jnp.float32)
        gate, up, sig = swish(pre_ref[i], hidden)
        act = gate * sig
        dot = jnp.sum(act * up * back, axis=1, keepdims=True)
        found = jnp.where(lane == first + i, dot, found)
        grad_up = back * act
        grad_gate = back * up * sig * (1.0 + gate * (1.0 - sig))
        kept.append(jnp.concatenate([grad_gate, grad_up], axis=1).astype(jnp.bfloat16))
    dots[...] = found
    for i in range(STEP):
        gate_up = w_ref[i, 0 : 2 * hidden, :]
        rows = jnp.dot(kept[i], gate_up, preferred_element_type=jnp.float32)
        keep(first + i, slots, rows.astype(jnp.bfloat16))

    @pl.when(first + STEP == half)
    def _():
        combine(rank_ref, slots, out_ref)
        low_rows = SLOTS // 2

        def one(s, carry):
            part = dots[pl.ds(pl.multiple_of(s * SLOTS, SLOTS), SLOTS), 0:half]
            high = part.astype(jnp.bfloat16).astype(jnp.float32)
            low = part - high
            blank = jnp.zeros((low_rows, model - 4 * half), jnp.float32)
            line = [high[0:low_rows], low[0:low_rows], high[low_rows:], low[low_rows:], blank]
            out_ref[s, tok : tok + low_rows, :] = jnp.concatenate(line, axis=1).astype(jnp.bfloat16)
            return carry

        lax.fori_loop(0, sources, one, 0)


def params():
    return pltpu.CompilerParams(dimension_semantics=("arbitrary",), vmem_limit_bytes=VMEM)


def each(e):
    return (e, 0, 0)


def whole(e):
    return (0, 0, 0)


def gather_rows(ranks, rows):
    sources, half, tok = ranks.shape
    model = rows.shape[2]
    return pl.pallas_call(
        gather_kernel,
        grid=(sources,),
        in_specs=[
            pl.BlockSpec((1, half, tok), each),
            pl.BlockSpec((1, rows.shape[1], model), each),
        ],
        out_specs=pl.BlockSpec((half, SLOTS, model), lambda s: (0, s, 0)),
        out_shape=jax.ShapeDtypeStruct((half, sources * SLOTS, model), jnp.bfloat16),
        compiler_params=params(),
        cost_estimate=pl.CostEstimate(
            flops=2 * sources * half * SLOTS * tok * model,
            bytes_accessed=2 * half * sources * SLOTS * model + 2 * rows.size,
            transcendentals=0,
        ),
        name="gather_rows",
    )(ranks, rows)


def forward(weights, x_rows, scales, ranks):
    half, w_rows, model = weights.shape
    hidden = w_rows // 3
    sources, _, tok = ranks.shape
    rows = sources * SLOTS
    return pl.pallas_call(
        forward_kernel,
        grid=(half // STEP,),
        in_specs=[
            pl.BlockSpec((STEP, w_rows, model), each),
            pl.BlockSpec((STEP, rows, model), each),
            pl.BlockSpec((STEP, 8, rows), each),
            pl.BlockSpec((sources, half, tok), whole),
        ],
        out_specs=[
            pl.BlockSpec((sources, tok, model), whole),
            pl.BlockSpec((STEP, rows, 2 * hidden), each),
        ],
        out_shape=[
            jax.ShapeDtypeStruct((sources, tok, model), jnp.bfloat16),
            jax.ShapeDtypeStruct((half, rows, 2 * hidden), jnp.float32),
        ],
        scratch_shapes=[
            pltpu.VMEM((sources, half * SLOTS, model), jnp.bfloat16),
        ],
        compiler_params=params(),
        cost_estimate=pl.CostEstimate(
            flops=6 * half * rows * hidden * model,
            bytes_accessed=2 * (weights.size + x_rows.size),
            transcendentals=half * rows * hidden,
        ),
        name="forward_experts",
    )(weights, x_rows, scales, ranks)


def backward(weights, pre, scales, ranks, cotangents):
    half, w_rows, model = weights.shape
    sources, _, tok = ranks.shape
    rows = sources * SLOTS
    out_rows = tok + SLOTS // 2
    return pl.pallas_call(
        backward_kernel,
        grid=(half // STEP,),
        in_specs=[
            pl.BlockSpec((STEP, w_rows, model), each),
            pl.BlockSpec((STEP, rows, pre.shape[2]), each),
            pl.BlockSpec((sources, 8, half * SLOTS), whole),
            pl.BlockSpec((sources, half, tok), whole),
            pl.BlockSpec((sources, tok, model), whole),
        ],
        out_specs=pl.BlockSpec((sources, out_rows, model), whole),
        out_shape=jax.ShapeDtypeStruct((sources, out_rows, model), jnp.bfloat16),
        scratch_shapes=[
            pltpu.VMEM((sources, half * SLOTS, model), jnp.bfloat16),
            pltpu.VMEM((rows, 128), jnp.float32),
        ],
        compiler_params=params(),
        cost_estimate=pl.CostEstimate(
            flops=6 * half * rows * (w_rows // 3) * model,
            bytes_accessed=2 * (weights.size + 2 * pre.size),
            transcendentals=half * rows * (w_rows // 3),
        ),
        name="backward_experts",
    )(weights, pre, scales, ranks, cotangents)


def body(tokens, expert_ids, router_gates, w_in, w_down, cotangent):
    tok, model = tokens.shape
    planes = lax.axis_size("dp")
    side = 4
    half = lax.axis_size("expert")
    experts = 2 * half
    parity = lax.rem(lax.axis_index("dp") // side, 2)

    def both_slices(which):
        pair = lax.dynamic_index_in_dim(w_in, which, 0, keepdims=False)
        down = lax.dynamic_slice_in_dim(w_down, which, 1, 0)
        return jnp.concatenate([pair, down], axis=0)

    swap = [(d, (((d // side) ^ 1) * side) + d % side) for d in range(planes)]
    other = lax.ppermute(both_slices(1 - parity), "dp", swap)
    mine = jnp.concatenate([both_slices(parity), other], axis=1).reshape(-1, model)
    weights = lax.all_gather(mine, "expert", axis=0, tiled=False)

    ids = expert_ids.T
    match = ids[:, None, :] == jnp.arange(experts, dtype=jnp.int32)[None, :, None]
    chosen = jnp.any(match, axis=0)
    gate_of = jnp.sum(jnp.where(match, router_gates.T[:, None, :], 0.0), axis=0)
    earlier = jnp.arange(tok)[:, None] < jnp.arange(tok)[None, :]
    rank = jnp.dot(
        chosen.astype(jnp.bfloat16), earlier.astype(jnp.bfloat16), preferred_element_type=jnp.float32
    )
    rank = jnp.where(chosen, rank, -1.0)
    slot_no = jnp.arange(SLOTS, dtype=jnp.float32)
    at_slot = rank[:, None, :] == slot_no[None, :, None]
    slot_gate = jnp.sum(jnp.where(at_slot, gate_of[:, None, :], 0.0), axis=2)
    gate_high = lax.reduce_precision(slot_gate, 8, 7)
    gate_low = slot_gate - gate_high

    def facts(odd):
        flat = lambda a: a.reshape(half, 2, -1)[:, odd].reshape(-1)
        return jnp.concatenate([flat(rank), flat(gate_high), flat(gate_low)]).astype(jnp.bfloat16)

    fact_rows = 8
    known = jnp.stack([facts(0), facts(1)])
    known = jnp.pad(known, ((0, 0), (0, fact_rows * model - known.shape[1])))
    known = known.reshape(2, 1, fact_rows, model)
    known = jnp.broadcast_to(known[:, None], (2, side, 1, fact_rows, model)).reshape(
        1, 2 * side, fact_rows, model
    )
    known = jnp.broadcast_to(known, (planes // (2 * side), 2 * side, fact_rows, model))
    known = known.reshape(planes, fact_rows, model)
    spread = lambda a: jnp.broadcast_to(a[None], (planes, tok, model))
    swap_rows = lambda a: lax.all_to_all(a, "dp", split_axis=0, concat_axis=0, tiled=True)
    rows = swap_rows(jnp.concatenate([spread(tokens), known], axis=1))
    cotangents = swap_rows(spread(cotangent))

    facts_in = rows[:, tok:, :].reshape(planes, fact_rows * model).astype(jnp.float32)
    first, second = half * tok, half * tok + half * SLOTS
    ranks = facts_in[:, 0:first].reshape(planes, half, tok)
    scales = facts_in[:, first:second] + facts_in[:, second : second + half * SLOTS]
    by_source = jnp.broadcast_to(scales[:, None], (planes, 8, half * SLOTS))
    scales = scales.reshape(planes, half, SLOTS).swapaxes(0, 1).reshape(half, 1, planes * SLOTS)
    scales = jnp.broadcast_to(scales, (half, 8, planes * SLOTS))

    x_rows = gather_rows(ranks, rows)
    layer_part, pre = forward(weights, x_rows, scales, ranks)
    layer_output = lax.psum_scatter(
        layer_part.reshape(planes * tok, model), "dp", scatter_dimension=0, tiled=True
    )
    grad_in = swap_rows(backward(weights, pre, by_source, ranks, cotangents)).astype(jnp.float32)
    token_grads = jnp.sum(grad_in[:, 0:tok], axis=0).astype(jnp.bfloat16)

    dots = grad_in[:, tok:, 0 : 4 * half].reshape(2, 2, side, SLOTS // 2, 2, 2, half)
    dots = jnp.sum(dots, axis=(0, 2, 5))
    dots = dots.transpose(3, 0, 2, 1).reshape(experts, SLOTS)
    by_expert = jnp.sum(jnp.where(at_slot, dots[:, :, None], 0.0), axis=1)
    gate_grads = jnp.sum(jnp.where(match, by_expert[None], 0.0), axis=1).T / router_gates
    return (layer_output, token_grads, gate_grads)


def solution(mesh):
    both = P(("dp", "expert"), None)
    placed = (both, both, both, P("expert", None, "dp", None), P("expert", "dp", None), both)
    return jax.shard_map(
        body, mesh=mesh, in_specs=placed, out_specs=(both, both, both), check_vma=False
    )
```

```python
import jax
import jax.numpy as jnp
from jax import lax
from jax.experimental import pallas as pl
from jax.experimental.pallas import tpu as pltpu
from jax.sharding import PartitionSpec as P

STEP = 8
SLOTS = 16
VMEM = 56 * 1024 * 1024
NT = (((1,), (1,)), ((), ()))
TN = (((0,), (0,)), ((), ()))


def one_hot(ranks, slot):
    group, tok = ranks.shape
    hit = jnp.where(ranks[:, None, :] == slot, 1.0, 0.0)
    return hit.reshape(group * SLOTS, tok).astype(jnp.bfloat16)


def slot_numbers(group, tok):
    return lax.broadcasted_iota(jnp.int32, (group, SLOTS, tok), 1).astype(jnp.float32)


def gather_kernel(rank_ref, rows_ref, x_ref):
    half, tok = rank_ref.shape[1:]
    pick = one_hot(rank_ref[0], slot_numbers(half, tok))
    xs = jnp.dot(pick, rows_ref[0, 0:tok, :], preferred_element_type=jnp.float32)
    x_ref[...] = xs.astype(jnp.bfloat16).reshape(x_ref.shape)


def keep(expert, slots_ref, rows):
    at = pl.multiple_of(expert * SLOTS, SLOTS)
    slots_ref[:, pl.ds(at, SLOTS), :] = rows.reshape(slots_ref.shape[0], SLOTS, rows.shape[1])


def combine(rank_ref, slots_ref, *out_refs):
    sources, half, tok = rank_ref.shape
    slot = slot_numbers(half, tok)

    def one(s, carry):
        place = one_hot(rank_ref[s], slot)
        sums = lax.dot_general(place, slots_ref[s], TN, preferred_element_type=jnp.float32)
        start = 0
        for out_ref in out_refs:
            stop = start + out_ref.shape[-1]
            part = sums[:, start:stop].astype(out_ref.dtype)
            if len(out_ref.shape) == 3:
                out_ref[s, 0:tok, :] = part
            else:
                side = out_ref.shape[0]
                out_ref[lax.rem(s, side), lax.div(s, side), 0:tok, :] = part
            start = stop
        return carry

    lax.fori_loop(0, sources, one, 0)


def swish(pre, hidden):
    gate = pre[:, 0:hidden]
    up = pre[:, hidden : 2 * hidden]
    sig = 1.0 / (1.0 + jnp.exp(-gate))
    return gate, up, sig


def forward_kernel(w_ref, x_ref, g_ref, rank_ref, out_ref, pre_ref, slots):
    hidden = w_ref.shape[1] // 3
    first = pl.program_id(0) * STEP
    kept = []
    for i in range(STEP):
        gate_up = w_ref[i, 0 : 2 * hidden, :]
        pre = lax.dot_general(x_ref[i], gate_up, NT, preferred_element_type=jnp.float32)
        pre_ref[i] = pre
        gate, up, sig = swish(pre, hidden)
        kept.append((gate * sig * up).astype(jnp.bfloat16))
    for i in range(STEP):
        down = w_ref[i, 2 * hidden : 3 * hidden, :]
        rows = jnp.dot(kept[i], down, preferred_element_type=jnp.float32)
        scale = jnp.transpose(g_ref[i])[:, 0:1]
        keep(first + i, slots, (rows * scale).astype(jnp.bfloat16))

    @pl.when(first + STEP == rank_ref.shape[1])
    def _():
        combine(rank_ref, slots, out_ref)


def backward_kernel(
    w_ref, pre_ref, g_ref, rank_ref, c_ref, out_ref, more_ref, slots, dots
):
    hidden = w_ref.shape[1] // 3
    first = pl.program_id(0) * STEP
    sources, tok, model = c_ref.shape
    half = rank_ref.shape[1]

    @pl.when(first == 0)
    def _():
        slot = slot_numbers(half, tok)

        def one(s, carry):
            cs = jnp.dot(one_hot(rank_ref[s], slot), c_ref[s], preferred_element_type=jnp.float32)
            scale = jnp.transpose(g_ref[s])[:, 0:1]
            slots[s] = (cs * scale).astype(jnp.bfloat16)
            return carry

        lax.fori_loop(0, sources, one, 0)
        dots[...] = jnp.zeros_like(dots)

    kept = []
    lane = lax.broadcasted_iota(jnp.int32, dots.shape, 1)
    found = dots[...]
    for i in range(STEP):
        down = w_ref[i, 2 * hidden : 3 * hidden, :]
        at = pl.multiple_of((first + i) * SLOTS, SLOTS)
        cs = slots[:, pl.ds(at, SLOTS), :].reshape(sources * SLOTS, model)
        back = lax.dot_general(cs, down, NT, preferred_element_type=jnp.float32)
        gate, up, sig = swish(pre_ref[i], hidden)
        act = gate * sig
        dot = jnp.sum(act * up * back, axis=1, keepdims=True)
        found = jnp.where(lane == first + i, dot, found)
        grad_up = back * act
        grad_gate = back * up * sig * (1.0 + gate * (1.0 - sig))
        kept.append(jnp.concatenate([grad_gate, grad_up], axis=1).astype(jnp.bfloat16))
    dots[...] = found
    for i in range(STEP):
        gate_up = w_ref[i, 0 : 2 * hidden, :]
        rows = jnp.dot(kept[i], gate_up, preferred_element_type=jnp.float32)
        keep(first + i, slots, rows.astype(jnp.bfloat16))

    @pl.when(first + STEP == half)
    def _():
        combine(rank_ref, slots, out_ref, more_ref)
        low_rows, side = SLOTS // 2, out_ref.shape[0]

        def one(s, carry):
            part = dots[pl.ds(pl.multiple_of(s * SLOTS, SLOTS), SLOTS), 0:half]
            high = part.astype(jnp.bfloat16).astype(jnp.float32)
            low = part - high
            blank = jnp.zeros((low_rows, out_ref.shape[3] - 4 * half), jnp.float32)
            line = [high[0:low_rows], low[0:low_rows], high[low_rows:], low[low_rows:], blank]
            line = jnp.concatenate(line, axis=1).astype(jnp.bfloat16)
            out_ref[lax.rem(s, side), lax.div(s, side), tok : tok + low_rows, :] = line
            return carry

        lax.fori_loop(0, sources, one, 0)


def params():
    return pltpu.CompilerParams(dimension_semantics=("arbitrary",), vmem_limit_bytes=VMEM)


def each(e):
    return (e, 0, 0)


def whole(e):
    return (0, 0, 0)


def gather_rows(ranks, rows):
    sources, half, tok = ranks.shape
    model = rows.shape[2]
    return pl.pallas_call(
        gather_kernel,
        grid=(sources,),
        in_specs=[
            pl.BlockSpec((1, half, tok), each),
            pl.BlockSpec((1, rows.shape[1], model), each),
        ],
        out_specs=pl.BlockSpec((half, SLOTS, model), lambda s: (0, s, 0)),
        out_shape=jax.ShapeDtypeStruct((half, sources * SLOTS, model), jnp.bfloat16),
        compiler_params=params(),
        cost_estimate=pl.CostEstimate(
            flops=2 * sources * half * SLOTS * tok * model,
            bytes_accessed=2 * half * sources * SLOTS * model + 2 * rows.size,
            transcendentals=0,
        ),
        name="gather_rows",
    )(ranks, rows)


def forward(weights, x_rows, scales, ranks):
    half, w_rows, model = weights.shape
    hidden = w_rows // 3
    sources, _, tok = ranks.shape
    rows = sources * SLOTS
    return pl.pallas_call(
        forward_kernel,
        grid=(half // STEP,),
        in_specs=[
            pl.BlockSpec((STEP, w_rows, model), each),
            pl.BlockSpec((STEP, rows, model), each),
            pl.BlockSpec((STEP, 8, rows), each),
            pl.BlockSpec((sources, half, tok), whole),
        ],
        out_specs=[
            pl.BlockSpec((sources, tok, model), whole),
            pl.BlockSpec((STEP, rows, 2 * hidden), each),
        ],
        out_shape=[
            jax.ShapeDtypeStruct((sources, tok, model), jnp.bfloat16),
            jax.ShapeDtypeStruct((half, rows, 2 * hidden), jnp.float32),
        ],
        scratch_shapes=[
            pltpu.VMEM((sources, half * SLOTS, model), jnp.bfloat16),
        ],
        compiler_params=params(),
        cost_estimate=pl.CostEstimate(
            flops=6 * half * rows * hidden * model,
            bytes_accessed=2 * (weights.size + x_rows.size),
            transcendentals=half * rows * hidden,
        ),
        name="forward_experts",
    )(weights, x_rows, scales, ranks)


def backward(weights, pre, scales, ranks, cotangents, side):
    half, w_rows, model = weights.shape
    sources, _, tok = ranks.shape
    rows = sources * SLOTS
    out_rows = tok + SLOTS // 2
    return pl.pallas_call(
        backward_kernel,
        grid=(half // STEP,),
        in_specs=[
            pl.BlockSpec((STEP, w_rows, model), each),
            pl.BlockSpec((STEP, rows, pre.shape[2]), each),
            pl.BlockSpec((sources, 8, half * SLOTS), whole),
            pl.BlockSpec((sources, half, tok), whole),
            pl.BlockSpec((sources, tok, model), whole),
        ],
        out_specs=[
            pl.BlockSpec((side, sources // side, out_rows, model // 2), lambda e: (0, 0, 0, 0)),
            pl.BlockSpec((side, sources // side, tok, model // 2), lambda e: (0, 0, 0, 0)),
        ],
        out_shape=[
            jax.ShapeDtypeStruct((side, sources // side, out_rows, model // 2), jnp.bfloat16),
            jax.ShapeDtypeStruct((side, sources // side, tok, model // 2), jnp.bfloat16),
        ],
        scratch_shapes=[
            pltpu.VMEM((sources, half * SLOTS, model), jnp.bfloat16),
            pltpu.VMEM((rows, 128), jnp.float32),
        ],
        compiler_params=params(),
        cost_estimate=pl.CostEstimate(
            flops=6 * half * rows * (w_rows // 3) * model,
            bytes_accessed=2 * (weights.size + 2 * pre.size),
            transcendentals=half * rows * (w_rows // 3),
        ),
        name="backward_experts",
    )(weights, pre, scales, ranks, cotangents)


def body(tokens, expert_ids, router_gates, w_in, w_down, cotangent):
    tok, model = tokens.shape
    planes = lax.axis_size("dp")
    side = 4
    half = lax.axis_size("expert")
    experts = 2 * half
    parity = lax.rem(lax.axis_index("dp") // side, 2)

    def both_slices(which):
        pair = lax.dynamic_index_in_dim(w_in, which, 0, keepdims=False)
        down = lax.dynamic_slice_in_dim(w_down, which, 1, 0)
        return jnp.concatenate([pair, down], axis=0)

    swap = [(d, (((d // side) ^ 1) * side) + d % side) for d in range(planes)]
    other = lax.ppermute(both_slices(1 - parity), "dp", swap)
    mine = jnp.concatenate([both_slices(parity), other], axis=1).reshape(-1, model)
    weights = lax.all_gather(mine, "expert", axis=0, tiled=False)

    ids = expert_ids.T
    match = ids[:, None, :] == jnp.arange(experts, dtype=jnp.int32)[None, :, None]
    chosen = jnp.any(match, axis=0)
    gate_of = jnp.sum(jnp.where(match, router_gates.T[:, None, :], 0.0), axis=0)
    earlier = jnp.arange(tok)[:, None] < jnp.arange(tok)[None, :]
    rank = jnp.dot(
        chosen.astype(jnp.bfloat16), earlier.astype(jnp.bfloat16), preferred_element_type=jnp.float32
    )
    rank = jnp.where(chosen, rank, -1.0)
    slot_no = jnp.arange(SLOTS, dtype=jnp.float32)
    at_slot = rank[:, None, :] == slot_no[None, :, None]
    slot_gate = jnp.sum(jnp.where(at_slot, gate_of[:, None, :], 0.0), axis=2)
    gate_high = lax.reduce_precision(slot_gate, 8, 7)
    gate_low = slot_gate - gate_high

    def facts(odd):
        flat = lambda a: a.reshape(half, 2, -1)[:, odd].reshape(-1)
        return jnp.concatenate([flat(rank), flat(gate_high), flat(gate_low)]).astype(jnp.bfloat16)

    fact_rows = 8
    known = jnp.stack([facts(0), facts(1)])
    known = jnp.pad(known, ((0, 0), (0, fact_rows * model - known.shape[1])))
    known = known.reshape(2, 1, fact_rows, model)
    known = jnp.broadcast_to(known[:, None], (2, side, 1, fact_rows, model)).reshape(
        1, 2 * side, fact_rows, model
    )
    known = jnp.broadcast_to(known, (planes // (2 * side), 2 * side, fact_rows, model))
    known = known.reshape(planes, fact_rows, model)
    spread = lambda a: jnp.broadcast_to(a[None], (planes, tok, model))
    swap_rows = lambda a: lax.all_to_all(a, "dp", split_axis=0, concat_axis=0, tiled=True)
    rows = swap_rows(jnp.concatenate([spread(tokens), known], axis=1))
    cotangents = swap_rows(spread(cotangent + 0.0 * rows[0, 0, 0]))

    facts_in = rows[:, tok:, :].reshape(planes, fact_rows * model).astype(jnp.float32)
    first, second = half * tok, half * tok + half * SLOTS
    ranks = facts_in[:, 0:first].reshape(planes, half, tok)
    scales = facts_in[:, first:second] + facts_in[:, second : second + half * SLOTS]
    by_source = jnp.broadcast_to(scales[:, None], (planes, 8, half * SLOTS))
    scales = scales.reshape(planes, half, SLOTS).swapaxes(0, 1).reshape(half, 1, planes * SLOTS)
    scales = jnp.broadcast_to(scales, (half, 8, planes * SLOTS))

    scales = scales + 0.0 * cotangents[0, 0, 0].astype(jnp.float32)
    x_rows = gather_rows(ranks, rows)
    layer_part, pre = forward(weights, x_rows, scales, ranks)
    along_x = [[x * side + y for x in range(planes // side)] for y in range(side)]
    along_y = [[x * side + y for y in range(side)] for x in range(planes // side)]

    def reduce_rows(a, groups):
        return lax.psum_scatter(
            a, "dp", scatter_dimension=0, axis_index_groups=groups, tiled=True
        )

    def swap_along(a, groups):
        return lax.all_to_all(
            a, "dp", split_axis=0, concat_axis=0, axis_index_groups=groups, tiled=True
        )

    layer_x = reduce_rows(layer_part.reshape(planes * tok, model), along_x)
    first_part, second_part = backward(weights, pre, by_source, ranks, cotangents, side)
    first_in = swap_along(first_part, along_y)
    layer_x = layer_x + 0.0 * first_in[0, 0, 0, 0]
    layer_output = reduce_rows(layer_x, along_y)
    second_in = swap_along(second_part + 0.0 * layer_x[0, 0], along_y)

    first_in = first_in.astype(jnp.float32)
    dots = jnp.sum(first_in[:, :, tok:, 0 : 4 * half], axis=0)
    dots = jnp.sum(dots.reshape(-1, SLOTS // 2, 2, 2, half), axis=3)
    high = lax.reduce_precision(dots, 8, 7)
    dots = jnp.stack([high, dots - high], axis=3).reshape(-1, SLOTS // 2, 4 * half)
    dots = jnp.pad(dots, ((0, 0), (0, 0), (0, model - 4 * half)))
    halves = [first_in[:, :, 0:tok], second_in.astype(jnp.float32)]
    grad_sums = jnp.concatenate([jnp.sum(a, axis=0) for a in halves], axis=2)
    grad_in = jnp.concatenate([grad_sums, dots], axis=1).astype(jnp.bfloat16)
    grad_in = swap_along(grad_in, along_x).astype(jnp.float32)
    token_grads = jnp.sum(grad_in[:, 0:tok], axis=0).astype(jnp.bfloat16)
    dots = grad_in[:, tok:, 0 : 4 * half].reshape(-1, 2, SLOTS // 2, 2, 2, half)
    dots = jnp.sum(dots, axis=(0, 4))
    dots = dots.transpose(3, 0, 2, 1).reshape(experts, SLOTS)
    by_expert = jnp.sum(jnp.where(at_slot, dots[:, :, None], 0.0), axis=1)
    gate_grads = jnp.sum(jnp.where(match, by_expert[None], 0.0), axis=1).T / router_gates
    return (layer_output, token_grads, gate_grads)


def solution(mesh):
    both = P(("dp", "expert"), None)
    placed = (both, both, both, P("expert", None, "dp", None), P("expert", "dp", None), both)
    return jax.shard_map(
        body, mesh=mesh, in_specs=placed, out_specs=(both, both, both), check_vma=False
    )
```

```python
import jax
import jax.numpy as jnp
from jax import lax
from jax.experimental import pallas as pl
from jax.experimental.pallas import tpu as pltpu
from jax.sharding import PartitionSpec as P

STEP = 8
SLOTS = 16
VMEM = 56 * 1024 * 1024
NT = (((1,), (1,)), ((), ()))
TN = (((0,), (0,)), ((), ()))


def one_hot(ranks, slot):
    group, tok = ranks.shape
    hit = jnp.where(ranks[:, None, :] == slot, 1.0, 0.0)
    return hit.reshape(group * SLOTS, tok).astype(jnp.bfloat16)


def slot_numbers(group, tok):
    return lax.broadcasted_iota(jnp.int32, (group, SLOTS, tok), 1).astype(jnp.float32)


def gather_kernel(rank_ref, rows_ref, x_ref):
    half, tok = rank_ref.shape[1:]
    pick = one_hot(rank_ref[0], slot_numbers(half, tok))
    xs = jnp.dot(pick, rows_ref[0, 0:tok, :], preferred_element_type=jnp.float32)
    x_ref[...] = xs.astype(jnp.bfloat16).reshape(x_ref.shape)


def keep(expert, slots_ref, rows):
    at = pl.multiple_of(expert * SLOTS, SLOTS)
    slots_ref[:, pl.ds(at, SLOTS), :] = rows.reshape(slots_ref.shape[0], SLOTS, rows.shape[1])


def combine(rank_ref, slots_ref, out_ref):
    sources, half, tok = rank_ref.shape
    slot = slot_numbers(half, tok)

    def one(s, carry):
        place = one_hot(rank_ref[s], slot)
        sums = lax.dot_general(place, slots_ref[s], TN, preferred_element_type=jnp.float32)
        if len(out_ref.shape) == 3:
            out_ref[s] = sums.astype(out_ref.dtype)
        else:
            side = out_ref.shape[0]
            out_ref[lax.rem(s, side), lax.div(s, side), 0:tok, :] = sums.astype(out_ref.dtype)
        return carry

    lax.fori_loop(0, sources, one, 0)


def swish(pre, hidden):
    gate = pre[:, 0:hidden]
    up = pre[:, hidden : 2 * hidden]
    sig = 1.0 / (1.0 + jnp.exp(-gate))
    return gate, up, sig


def forward_kernel(w_ref, x_ref, g_ref, rank_ref, out_ref, pre_ref, slots):
    hidden = w_ref.shape[1] // 3
    first = pl.program_id(0) * STEP
    kept = []
    for i in range(STEP):
        gate_up = w_ref[i, 0 : 2 * hidden, :]
        pre = lax.dot_general(x_ref[i], gate_up, NT, preferred_element_type=jnp.float32)
        pre_ref[i] = pre
        gate, up, sig = swish(pre, hidden)
        kept.append((gate * sig * up).astype(jnp.bfloat16))
    for i in range(STEP):
        down = w_ref[i, 2 * hidden : 3 * hidden, :]
        rows = jnp.dot(kept[i], down, preferred_element_type=jnp.float32)
        scale = jnp.transpose(g_ref[i])[:, 0:1]
        keep(first + i, slots, (rows * scale).astype(jnp.bfloat16))

    @pl.when(first + STEP == rank_ref.shape[1])
    def _():
        combine(rank_ref, slots, out_ref)


def backward_kernel(w_ref, pre_ref, g_ref, rank_ref, c_ref, out_ref, slots, dots):
    hidden = w_ref.shape[1] // 3
    first = pl.program_id(0) * STEP
    sources, tok, model = c_ref.shape
    half = rank_ref.shape[1]

    @pl.when(first == 0)
    def _():
        slot = slot_numbers(half, tok)

        def one(s, carry):
            cs = jnp.dot(one_hot(rank_ref[s], slot), c_ref[s], preferred_element_type=jnp.float32)
            scale = jnp.transpose(g_ref[s])[:, 0:1]
            slots[s] = (cs * scale).astype(jnp.bfloat16)
            return carry

        lax.fori_loop(0, sources, one, 0)
        dots[...] = jnp.zeros_like(dots)

    kept = []
    lane = lax.broadcasted_iota(jnp.int32, dots.shape, 1)
    found = dots[...]
    for i in range(STEP):
        down = w_ref[i, 2 * hidden : 3 * hidden, :]
        at = pl.multiple_of((first + i) * SLOTS, SLOTS)
        cs = slots[:, pl.ds(at, SLOTS), :].reshape(sources * SLOTS, model)
        back = lax.dot_general(cs, down, NT, preferred_element_type=jnp.float32)
        gate, up, sig = swish(pre_ref[i], hidden)
        act = gate * sig
        dot = jnp.sum(act * up * back, axis=1, keepdims=True)
        found = jnp.where(lane == first + i, dot, found)
        grad_up = back * act
        grad_gate = back * up * sig * (1.0 + gate * (1.0 - sig))
        kept.append(jnp.concatenate([grad_gate, grad_up], axis=1).astype(jnp.bfloat16))
    dots[...] = found
    for i in range(STEP):
        gate_up = w_ref[i, 0 : 2 * hidden, :]
        rows = jnp.dot(kept[i], gate_up, preferred_element_type=jnp.float32)
        keep(first + i, slots, rows.astype(jnp.bfloat16))

    @pl.when(first + STEP == half)
    def _():
        combine(rank_ref, slots, out_ref)
        low_rows, side = SLOTS // 2, out_ref.shape[0]

        def one(s, carry):
            part = dots[pl.ds(pl.multiple_of(s * SLOTS, SLOTS), SLOTS), 0:half]
            high = part.astype(jnp.bfloat16).astype(jnp.float32)
            low = part - high
            blank = jnp.zeros((low_rows, out_ref.shape[3] - 4 * half), jnp.float32)
            line = [high[0:low_rows], low[0:low_rows], high[low_rows:], low[low_rows:], blank]
            line = jnp.concatenate(line, axis=1).astype(jnp.bfloat16)
            out_ref[lax.rem(s, side), lax.div(s, side), tok : tok + low_rows, :] = line
            return carry

        lax.fori_loop(0, sources, one, 0)


def params():
    return pltpu.CompilerParams(dimension_semantics=("arbitrary",), vmem_limit_bytes=VMEM)


def each(e):
    return (e, 0, 0)


def whole(e):
    return (0, 0, 0)


def gather_rows(ranks, rows):
    sources, half, tok = ranks.shape
    model = rows.shape[2]
    return pl.pallas_call(
        gather_kernel,
        grid=(sources,),
        in_specs=[
            pl.BlockSpec((1, half, tok), each),
            pl.BlockSpec((1, rows.shape[1], model), each),
        ],
        out_specs=pl.BlockSpec((half, SLOTS, model), lambda s: (0, s, 0)),
        out_shape=jax.ShapeDtypeStruct((half, sources * SLOTS, model), jnp.bfloat16),
        compiler_params=params(),
        cost_estimate=pl.CostEstimate(
            flops=2 * sources * half * SLOTS * tok * model,
            bytes_accessed=2 * half * sources * SLOTS * model + 2 * rows.size,
            transcendentals=0,
        ),
        name="gather_rows",
    )(ranks, rows)


def forward(weights, x_rows, scales, ranks):
    half, w_rows, model = weights.shape
    hidden = w_rows // 3
    sources, _, tok = ranks.shape
    rows = sources * SLOTS
    return pl.pallas_call(
        forward_kernel,
        grid=(half // STEP,),
        in_specs=[
            pl.BlockSpec((STEP, w_rows, model), each),
            pl.BlockSpec((STEP, rows, model), each),
            pl.BlockSpec((STEP, 8, rows), each),
            pl.BlockSpec((sources, half, tok), whole),
        ],
        out_specs=[
            pl.BlockSpec((sources, tok, model), whole),
            pl.BlockSpec((STEP, rows, 2 * hidden), each),
        ],
        out_shape=[
            jax.ShapeDtypeStruct((sources, tok, model), jnp.bfloat16),
            jax.ShapeDtypeStruct((half, rows, 2 * hidden), jnp.float32),
        ],
        scratch_shapes=[
            pltpu.VMEM((sources, half * SLOTS, model), jnp.bfloat16),
        ],
        compiler_params=params(),
        cost_estimate=pl.CostEstimate(
            flops=6 * half * rows * hidden * model,
            bytes_accessed=2 * (weights.size + x_rows.size),
            transcendentals=half * rows * hidden,
        ),
        name="forward_experts",
    )(weights, x_rows, scales, ranks)


def backward(weights, pre, scales, ranks, cotangents, side):
    half, w_rows, model = weights.shape
    sources, _, tok = ranks.shape
    rows = sources * SLOTS
    out_rows = tok + SLOTS // 2
    return pl.pallas_call(
        backward_kernel,
        grid=(half // STEP,),
        in_specs=[
            pl.BlockSpec((STEP, w_rows, model), each),
            pl.BlockSpec((STEP, rows, pre.shape[2]), each),
            pl.BlockSpec((sources, 8, half * SLOTS), whole),
            pl.BlockSpec((sources, half, tok), whole),
            pl.BlockSpec((sources, tok, model), whole),
        ],
        out_specs=pl.BlockSpec((side, sources // side, out_rows, model), lambda e: (0, 0, 0, 0)),
        out_shape=jax.ShapeDtypeStruct((side, sources // side, out_rows, model), jnp.bfloat16),
        scratch_shapes=[
            pltpu.VMEM((sources, half * SLOTS, model), jnp.bfloat16),
            pltpu.VMEM((rows, 128), jnp.float32),
        ],
        compiler_params=params(),
        cost_estimate=pl.CostEstimate(
            flops=60 * half * rows * (w_rows // 3) * model,
            bytes_accessed=2 * (weights.size + 2 * pre.size),
            transcendentals=half * rows * (w_rows // 3),
        ),
        name="backward_experts",
    )(weights, pre, scales, ranks, cotangents)


def body(tokens, expert_ids, router_gates, w_in, w_down, cotangent):
    tok, model = tokens.shape
    planes = lax.axis_size("dp")
    side = 4
    half = lax.axis_size("expert")
    experts = 2 * half
    parity = lax.rem(lax.axis_index("dp") // side, 2)

    def both_slices(which):
        pair = lax.dynamic_index_in_dim(w_in, which, 0, keepdims=False)
        down = lax.dynamic_slice_in_dim(w_down, which, 1, 0)
        return jnp.concatenate([pair, down], axis=0)

    swap = [(d, (((d // side) ^ 1) * side) + d % side) for d in range(planes)]
    other = lax.ppermute(both_slices(1 - parity), "dp", swap)
    mine = jnp.concatenate([both_slices(parity), other], axis=1).reshape(-1, model)
    weights = lax.all_gather(mine, "expert", axis=0, tiled=False)

    ids = expert_ids.T
    match = ids[:, None, :] == jnp.arange(experts, dtype=jnp.int32)[None, :, None]
    chosen = jnp.any(match, axis=0)
    gate_of = jnp.sum(jnp.where(match, router_gates.T[:, None, :], 0.0), axis=0)
    earlier = jnp.arange(tok)[:, None] < jnp.arange(tok)[None, :]
    rank = jnp.dot(
        chosen.astype(jnp.bfloat16), earlier.astype(jnp.bfloat16), preferred_element_type=jnp.float32
    )
    rank = jnp.where(chosen, rank, -1.0)
    slot_no = jnp.arange(SLOTS, dtype=jnp.float32)
    at_slot = rank[:, None, :] == slot_no[None, :, None]
    slot_gate = jnp.sum(jnp.where(at_slot, gate_of[:, None, :], 0.0), axis=2)
    gate_high = lax.reduce_precision(slot_gate, 8, 7)
    gate_low = slot_gate - gate_high

    def facts(odd):
        flat = lambda a: a.reshape(half, 2, -1)[:, odd].reshape(-1)
        return jnp.concatenate([flat(rank), flat(gate_high), flat(gate_low)]).astype(jnp.bfloat16)

    fact_rows = 8
    known = jnp.stack([facts(0), facts(1)])
    known = jnp.pad(known, ((0, 0), (0, fact_rows * model - known.shape[1])))
    known = known.reshape(2, 1, fact_rows, model)
    known = jnp.broadcast_to(known[:, None], (2, side, 1, fact_rows, model)).reshape(
        1, 2 * side, fact_rows, model
    )
    known = jnp.broadcast_to(known, (planes // (2 * side), 2 * side, fact_rows, model))
    known = known.reshape(planes, fact_rows, model)
    spread = lambda a: jnp.broadcast_to(a[None], (planes, tok, model))
    swap_rows = lambda a: lax.all_to_all(a, "dp", split_axis=0, concat_axis=0, tiled=True)
    rows = swap_rows(jnp.concatenate([spread(tokens), known], axis=1))
    cotangents = swap_rows(spread(cotangent))

    facts_in = rows[:, tok:, :].reshape(planes, fact_rows * model).astype(jnp.float32)
    first, second = half * tok, half * tok + half * SLOTS
    ranks = facts_in[:, 0:first].reshape(planes, half, tok)
    scales = facts_in[:, first:second] + facts_in[:, second : second + half * SLOTS]
    by_source = jnp.broadcast_to(scales[:, None], (planes, 8, half * SLOTS))
    scales = scales.reshape(planes, half, SLOTS).swapaxes(0, 1).reshape(half, 1, planes * SLOTS)
    scales = jnp.broadcast_to(scales, (half, 8, planes * SLOTS))

    x_rows = gather_rows(ranks, rows)
    layer_part, pre = forward(weights, x_rows, scales, ranks)
    along_x = [[x * side + y for x in range(planes // side)] for y in range(side)]
    along_y = [[x * side + y for y in range(side)] for x in range(planes // side)]

    def reduce_rows(a, groups):
        return lax.psum_scatter(
            a, "dp", scatter_dimension=0, axis_index_groups=groups, tiled=True
        )

    def swap_along(a, groups):
        return lax.all_to_all(
            a, "dp", split_axis=0, concat_axis=0, axis_index_groups=groups, tiled=True
        )

    layer_x = reduce_rows(layer_part.reshape(planes * tok, model), along_x)
    grad_part = backward(weights, pre, by_source, ranks, cotangents, side)
    layer_output = reduce_rows(layer_x, along_y)
    grad_in = swap_along(grad_part, along_y).astype(jnp.float32)

    dots = jnp.sum(grad_in[:, :, tok:, 0 : 4 * half], axis=0)
    dots = jnp.sum(dots.reshape(-1, SLOTS // 2, 2, 2, half), axis=3)
    high = lax.reduce_precision(dots, 8, 7)
    dots = jnp.stack([high, dots - high], axis=3).reshape(-1, SLOTS // 2, 4 * half)
    dots = jnp.pad(dots, ((0, 0), (0, 0), (0, model - 4 * half)))
    dots = dots + 0.0 * layer_output[0, 0].astype(jnp.float32)
    grad_sums = jnp.sum(grad_in[:, :, 0:tok], axis=0)
    grad_in = jnp.concatenate([grad_sums, dots], axis=1).astype(jnp.bfloat16)
    grad_in = swap_along(grad_in, along_x).astype(jnp.float32)
    token_grads = jnp.sum(grad_in[:, 0:tok], axis=0).astype(jnp.bfloat16)
    dots = grad_in[:, tok:, 0 : 4 * half].reshape(-1, 2, SLOTS // 2, 2, 2, half)
    dots = jnp.sum(dots, axis=(0, 4))
    dots = dots.transpose(3, 0, 2, 1).reshape(experts, SLOTS)
    by_expert = jnp.sum(jnp.where(at_slot, dots[:, :, None], 0.0), axis=1)
    gate_grads = jnp.sum(jnp.where(match, by_expert[None], 0.0), axis=1).T / router_gates
    return (layer_output, token_grads, gate_grads)


def solution(mesh):
    both = P(("dp", "expert"), None)
    placed = (both, both, both, P("expert", None, "dp", None), P("expert", "dp", None), both)
    return jax.shard_map(
        body, mesh=mesh, in_specs=placed, out_specs=(both, both, both), check_vma=False
    )
```

```python
import jax
import jax.numpy as jnp
from jax import lax
from jax.experimental import pallas as pl
from jax.experimental.pallas import tpu as pltpu
from jax.sharding import PartitionSpec as P

STEP = 8
SLOTS = 16
VMEM = 56 * 1024 * 1024
NT = (((1,), (1,)), ((), ()))
TN = (((0,), (0,)), ((), ()))


def one_hot(ranks, slot):
    group, tok = ranks.shape
    hit = jnp.where(ranks[:, None, :] == slot, 1.0, 0.0)
    return hit.reshape(group * SLOTS, tok).astype(jnp.bfloat16)


def slot_numbers(group, tok):
    return lax.broadcasted_iota(jnp.int32, (group, SLOTS, tok), 1).astype(jnp.float32)


def gather_kernel(rank_ref, rows_ref, x_ref):
    half, tok = rank_ref.shape[1:]
    pick = one_hot(rank_ref[0], slot_numbers(half, tok))
    xs = jnp.dot(pick, rows_ref[0, 0:tok, :], preferred_element_type=jnp.float32)
    x_ref[...] = xs.astype(jnp.bfloat16).reshape(x_ref.shape)


def keep(expert, slots_ref, rows):
    at = pl.multiple_of(expert * SLOTS, SLOTS)
    slots_ref[:, pl.ds(at, SLOTS), :] = rows.reshape(slots_ref.shape[0], SLOTS, rows.shape[1])


def combine(rank_ref, slots_ref, out_ref):
    sources, half, tok = rank_ref.shape
    slot = slot_numbers(half, tok)

    def one(s, carry):
        place = one_hot(rank_ref[s], slot)
        sums = lax.dot_general(place, slots_ref[s], TN, preferred_element_type=jnp.float32)
        out_ref[s, 0:tok, :] = sums.astype(out_ref.dtype)
        return carry

    lax.fori_loop(0, sources, one, 0)


def swish(pre, hidden):
    gate = pre[:, 0:hidden]
    up = pre[:, hidden : 2 * hidden]
    sig = 1.0 / (1.0 + jnp.exp(-gate))
    return gate, up, sig


def forward_kernel(w_ref, x_ref, g_ref, rank_ref, out_ref, pre_ref, slots):
    hidden = w_ref.shape[1] // 3
    first = pl.program_id(0) * STEP
    kept = []
    for i in range(STEP):
        gate_up = w_ref[i, 0 : 2 * hidden, :]
        pre = lax.dot_general(x_ref[i], gate_up, NT, preferred_element_type=jnp.float32)
        pre_ref[i] = pre
        gate, up, sig = swish(pre, hidden)
        kept.append((gate * sig * up).astype(jnp.bfloat16))
    for i in range(STEP):
        down = w_ref[i, 2 * hidden : 3 * hidden, :]
        rows = jnp.dot(kept[i], down, preferred_element_type=jnp.float32)
        scale = jnp.transpose(g_ref[i])[:, 0:1]
        keep(first + i, slots, (rows * scale).astype(jnp.bfloat16))

    @pl.when(first + STEP == rank_ref.shape[1])
    def _():
        combine(rank_ref, slots, out_ref)


def backward_kernel(w_ref, pre_ref, g_ref, rank_ref, c_ref, out_ref, slots, dots):
    hidden = w_ref.shape[1] // 3
    first = pl.program_id(0) * STEP
    sources, tok, model = c_ref.shape
    half = rank_ref.shape[1]

    @pl.when(first == 0)
    def _():
        slot = slot_numbers(half, tok)

        def one(s, carry):
            cs = jnp.dot(one_hot(rank_ref[s], slot), c_ref[s], preferred_element_type=jnp.float32)
            scale = jnp.transpose(g_ref[s])[:, 0:1]
            slots[s] = (cs * scale).astype(jnp.bfloat16)
            return carry

        lax.fori_loop(0, sources, one, 0)
        dots[...] = jnp.zeros_like(dots)

    kept = []
    lane = lax.broadcasted_iota(jnp.int32, dots.shape, 1)
    found = dots[...]
    for i in range(STEP):
        down = w_ref[i, 2 * hidden : 3 * hidden, :]
        at = pl.multiple_of((first + i) * SLOTS, SLOTS)
        cs = slots[:, pl.ds(at, SLOTS), :].reshape(sources * SLOTS, model)
        back = lax.dot_general(cs, down, NT, preferred_element_type=jnp.float32)
        gate, up, sig = swish(pre_ref[i], hidden)
        act = gate * sig
        dot = jnp.sum(act * up * back, axis=1, keepdims=True)
        found = jnp.where(lane == first + i, dot, found)
        grad_up = back * act
        grad_gate = back * up * sig * (1.0 + gate * (1.0 - sig))
        kept.append(jnp.concatenate([grad_gate, grad_up], axis=1).astype(jnp.bfloat16))
    dots[...] = found
    for i in range(STEP):
        gate_up = w_ref[i, 0 : 2 * hidden, :]
        rows = jnp.dot(kept[i], gate_up, preferred_element_type=jnp.float32)
        keep(first + i, slots, rows.astype(jnp.bfloat16))

    @pl.when(first + STEP == half)
    def _():
        combine(rank_ref, slots, out_ref)
        low_rows = SLOTS // 2

        def one(s, carry):
            part = dots[pl.ds(pl.multiple_of(s * SLOTS, SLOTS), SLOTS), 0:half]
            high = part.astype(jnp.bfloat16).astype(jnp.float32)
            low = part - high
            blank = jnp.zeros((low_rows, model - 4 * half), jnp.float32)
            line = [high[0:low_rows], low[0:low_rows], high[low_rows:], low[low_rows:], blank]
            out_ref[s, tok : tok + low_rows, :] = jnp.concatenate(line, axis=1).astype(jnp.bfloat16)
            return carry

        lax.fori_loop(0, sources, one, 0)


def params():
    return pltpu.CompilerParams(dimension_semantics=("arbitrary",), vmem_limit_bytes=VMEM)


def each(e):
    return (e, 0, 0)


def whole(e):
    return (0, 0, 0)


def gather_rows(ranks, rows):
    sources, half, tok = ranks.shape
    model = rows.shape[2]
    return pl.pallas_call(
        gather_kernel,
        grid=(sources,),
        in_specs=[
            pl.BlockSpec((1, half, tok), each),
            pl.BlockSpec((1, rows.shape[1], model), each),
        ],
        out_specs=pl.BlockSpec((half, SLOTS, model), lambda s: (0, s, 0)),
        out_shape=jax.ShapeDtypeStruct((half, sources * SLOTS, model), jnp.bfloat16),
        compiler_params=params(),
        cost_estimate=pl.CostEstimate(
            flops=2 * sources * half * SLOTS * tok * model,
            bytes_accessed=2 * half * sources * SLOTS * model + 2 * rows.size,
            transcendentals=0,
        ),
        name="gather_rows",
    )(ranks, rows)


def forward(weights, x_rows, scales, ranks):
    half, w_rows, model = weights.shape
    hidden = w_rows // 3
    sources, _, tok = ranks.shape
    rows = sources * SLOTS
    return pl.pallas_call(
        forward_kernel,
        grid=(half // STEP,),
        in_specs=[
            pl.BlockSpec((STEP, w_rows, model), each),
            pl.BlockSpec((STEP, rows, model), each),
            pl.BlockSpec((STEP, 8, rows), each),
            pl.BlockSpec((sources, half, tok), whole),
        ],
        out_specs=[
            pl.BlockSpec((sources, tok, model), whole),
            pl.BlockSpec((STEP, rows, 2 * hidden), each),
        ],
        out_shape=[
            jax.ShapeDtypeStruct((sources, tok, model), jnp.bfloat16),
            jax.ShapeDtypeStruct((half, rows, 2 * hidden), jnp.float32),
        ],
        scratch_shapes=[
            pltpu.VMEM((sources, half * SLOTS, model), jnp.bfloat16),
        ],
        compiler_params=params(),
        cost_estimate=pl.CostEstimate(
            flops=6 * half * rows * hidden * model,
            bytes_accessed=2 * (weights.size + x_rows.size),
            transcendentals=half * rows * hidden,
        ),
        name="forward_experts",
    )(weights, x_rows, scales, ranks)


def backward(weights, pre, scales, ranks, cotangents):
    half, w_rows, model = weights.shape
    sources, _, tok = ranks.shape
    rows = sources * SLOTS
    out_rows = tok + SLOTS // 2
    return pl.pallas_call(
        backward_kernel,
        grid=(half // STEP,),
        in_specs=[
            pl.BlockSpec((STEP, w_rows, model), each),
            pl.BlockSpec((STEP, rows, pre.shape[2]), each),
            pl.BlockSpec((sources, 8, half * SLOTS), whole),
            pl.BlockSpec((sources, half, tok), whole),
            pl.BlockSpec((sources, tok, model), whole),
        ],
        out_specs=pl.BlockSpec((sources, out_rows, model), whole),
        out_shape=jax.ShapeDtypeStruct((sources, out_rows, model), jnp.bfloat16),
        scratch_shapes=[
            pltpu.VMEM((sources, half * SLOTS, model), jnp.bfloat16),
            pltpu.VMEM((rows, 128), jnp.float32),
        ],
        compiler_params=params(),
        cost_estimate=pl.CostEstimate(
            flops=60 * half * rows * (w_rows // 3) * model,
            bytes_accessed=2 * (weights.size + 2 * pre.size),
            transcendentals=half * rows * (w_rows // 3),
        ),
        name="backward_experts",
    )(weights, pre, scales, ranks, cotangents)


def body(tokens, expert_ids, router_gates, w_in, w_down, cotangent):
    tok, model = tokens.shape
    planes = lax.axis_size("dp")
    side = 4
    half = lax.axis_size("expert")
    experts = 2 * half
    parity = lax.rem(lax.axis_index("dp") // side, 2)

    def both_slices(which):
        pair = lax.dynamic_index_in_dim(w_in, which, 0, keepdims=False)
        down = lax.dynamic_slice_in_dim(w_down, which, 1, 0)
        return jnp.concatenate([pair, down], axis=0)

    swap = [(d, (((d // side) ^ 1) * side) + d % side) for d in range(planes)]
    other = lax.ppermute(both_slices(1 - parity), "dp", swap)
    mine = jnp.concatenate([both_slices(parity), other], axis=1).reshape(-1, model)
    weights = lax.all_gather(mine, "expert", axis=0, tiled=False)

    ids = expert_ids.T
    match = ids[:, None, :] == jnp.arange(experts, dtype=jnp.int32)[None, :, None]
    chosen = jnp.any(match, axis=0)
    gate_of = jnp.sum(jnp.where(match, router_gates.T[:, None, :], 0.0), axis=0)
    earlier = jnp.arange(tok)[:, None] < jnp.arange(tok)[None, :]
    rank = jnp.dot(
        chosen.astype(jnp.bfloat16), earlier.astype(jnp.bfloat16), preferred_element_type=jnp.float32
    )
    rank = jnp.where(chosen, rank, -1.0)
    slot_no = jnp.arange(SLOTS, dtype=jnp.float32)
    at_slot = rank[:, None, :] == slot_no[None, :, None]
    slot_gate = jnp.sum(jnp.where(at_slot, gate_of[:, None, :], 0.0), axis=2)
    gate_high = lax.reduce_precision(slot_gate, 8, 7)
    gate_low = slot_gate - gate_high

    def facts(odd):
        flat = lambda a: a.reshape(half, 2, -1)[:, odd].reshape(-1)
        return jnp.concatenate([flat(rank), flat(gate_high), flat(gate_low)]).astype(jnp.bfloat16)

    fact_rows = 8
    known = jnp.stack([facts(0), facts(1)])
    known = jnp.pad(known, ((0, 0), (0, fact_rows * model - known.shape[1])))
    known = known.reshape(2, 1, fact_rows, model)
    known = jnp.broadcast_to(known[:, None], (2, side, 1, fact_rows, model)).reshape(
        1, 2 * side, fact_rows, model
    )
    known = jnp.broadcast_to(known, (planes // (2 * side), 2 * side, fact_rows, model))
    known = known.reshape(planes, fact_rows, model)
    spread = lambda a: jnp.broadcast_to(a[None], (planes, tok, model))
    swap_rows = lambda a: lax.all_to_all(a, "dp", split_axis=0, concat_axis=0, tiled=True)
    rows = swap_rows(jnp.concatenate([spread(tokens), known], axis=1))
    cotangents = swap_rows(spread(cotangent))

    facts_in = rows[:, tok:, :].reshape(planes, fact_rows * model).astype(jnp.float32)
    first, second = half * tok, half * tok + half * SLOTS
    ranks = facts_in[:, 0:first].reshape(planes, half, tok)
    scales = facts_in[:, first:second] + facts_in[:, second : second + half * SLOTS]
    by_source = jnp.broadcast_to(scales[:, None], (planes, 8, half * SLOTS))
    scales = scales.reshape(planes, half, SLOTS).swapaxes(0, 1).reshape(half, 1, planes * SLOTS)
    scales = jnp.broadcast_to(scales, (half, 8, planes * SLOTS))

    x_rows = gather_rows(ranks, rows)
    layer_part, pre = forward(weights, x_rows, scales, ranks)
    along_x = [[x * side + y for x in range(planes // side)] for y in range(side)]
    along_y = [[x * side + y for y in range(side)] for x in range(planes // side)]
    grad_part = backward(weights, pre, by_source, ranks, cotangents)
    layer_output = layer_part.reshape(planes * tok, model)
    for groups in (along_x, along_y):
        layer_output = lax.psum_scatter(
            layer_output, "dp", scatter_dimension=0, axis_index_groups=groups, tiled=True
        )
    grad_in = swap_rows(grad_part).astype(jnp.float32)
    token_grads = jnp.sum(grad_in[:, 0:tok], axis=0).astype(jnp.bfloat16)

    dots = grad_in[:, tok:, 0 : 4 * half].reshape(2, 2, side, SLOTS // 2, 2, 2, half)
    dots = jnp.sum(dots, axis=(0, 2, 5))
    dots = dots.transpose(3, 0, 2, 1).reshape(experts, SLOTS)
    by_expert = jnp.sum(jnp.where(at_slot, dots[:, :, None], 0.0), axis=1)
    gate_grads = jnp.sum(jnp.where(match, by_expert[None], 0.0), axis=1).T / router_gates
    return (layer_output, token_grads, gate_grads)


def solution(mesh):
    both = P(("dp", "expert"), None)
    placed = (both, both, both, P("expert", None, "dp", None), P("expert", "dp", None), both)
    return jax.shard_map(
        body, mesh=mesh, in_specs=placed, out_specs=(both, both, both), check_vma=False
    )
```

```python
import jax
import jax.numpy as jnp
from jax import lax
from jax.experimental import pallas as pl
from jax.experimental.pallas import tpu as pltpu
from jax.sharding import PartitionSpec as P

STEP = 8
SLOTS = 16
VMEM = 56 * 1024 * 1024
NT = (((1,), (1,)), ((), ()))
TN = (((0,), (0,)), ((), ()))


def one_hot(ranks, slot):
    group, tok = ranks.shape
    hit = jnp.where(ranks[:, None, :] == slot, 1.0, 0.0)
    return hit.reshape(group * SLOTS, tok).astype(jnp.bfloat16)


def slot_numbers(group, tok):
    return lax.broadcasted_iota(jnp.int32, (group, SLOTS, tok), 1).astype(jnp.float32)


def gather_kernel(rank_ref, rows_ref, x_ref):
    half, tok = rank_ref.shape[1:]
    pick = one_hot(rank_ref[0], slot_numbers(half, tok))
    xs = jnp.dot(pick, rows_ref[0, 0:tok, :], preferred_element_type=jnp.float32)
    x_ref[...] = xs.astype(jnp.bfloat16).reshape(x_ref.shape)


def keep(expert, slots_ref, rows):
    at = pl.multiple_of(expert * SLOTS, SLOTS)
    slots_ref[:, pl.ds(at, SLOTS), :] = rows.reshape(slots_ref.shape[0], SLOTS, rows.shape[1])


def combine(rank_ref, slots_ref, out_ref):
    sources, half, tok = rank_ref.shape
    slot = slot_numbers(half, tok)

    def one(s, carry):
        place = one_hot(rank_ref[s], slot)
        sums = lax.dot_general(place, slots_ref[s], TN, preferred_element_type=jnp.float32)
        out_ref[s, 0:tok, :] = sums.astype(out_ref.dtype)
        return carry

    lax.fori_loop(0, sources, one, 0, unroll=4)


def swish(pre, hidden):
    gate = pre[:, 0:hidden]
    up = pre[:, hidden : 2 * hidden]
    sig = 1.0 / (1.0 + jnp.exp(-gate))
    return gate, up, sig


def forward_kernel(w_ref, x_ref, g_ref, rank_ref, out_ref, pre_ref, slots):
    hidden = w_ref.shape[1] // 3
    first = pl.program_id(0) * STEP
    kept = []
    for i in range(STEP):
        gate_up = w_ref[i, 0 : 2 * hidden, :]
        pre = lax.dot_general(x_ref[i], gate_up, NT, preferred_element_type=jnp.float32)
        pre_ref[i] = pre
        gate, up, sig = swish(pre, hidden)
        kept.append((gate * sig * up).astype(jnp.bfloat16))
    for i in range(STEP):
        down = w_ref[i, 2 * hidden : 3 * hidden, :]
        rows = jnp.dot(kept[i], down, preferred_element_type=jnp.float32)
        scale = jnp.transpose(g_ref[i])[:, 0:1]
        keep(first + i, slots, (rows * scale).astype(jnp.bfloat16))

    @pl.when(first + STEP == rank_ref.shape[1])
    def _():
        combine(rank_ref, slots, out_ref)


def backward_kernel(w_ref, pre_ref, g_ref, rank_ref, c_ref, out_ref, slots, dots):
    hidden = w_ref.shape[1] // 3
    first = pl.program_id(0) * STEP
    sources, tok, model = c_ref.shape
    half = rank_ref.shape[1]

    @pl.when(first == 0)
    def _():
        slot = slot_numbers(half, tok)

        def one(s, carry):
            cs = jnp.dot(one_hot(rank_ref[s], slot), c_ref[s], preferred_element_type=jnp.float32)
            scale = jnp.transpose(g_ref[s])[:, 0:1]
            slots[s] = (cs * scale).astype(jnp.bfloat16)
            return carry

        lax.fori_loop(0, sources, one, 0, unroll=4)
        dots[...] = jnp.zeros_like(dots)

    kept = []
    lane = lax.broadcasted_iota(jnp.int32, dots.shape, 1)
    found = dots[...]
    for i in range(STEP):
        down = w_ref[i, 2 * hidden : 3 * hidden, :]
        at = pl.multiple_of((first + i) * SLOTS, SLOTS)
        cs = slots[:, pl.ds(at, SLOTS), :].reshape(sources * SLOTS, model)
        back = lax.dot_general(cs, down, NT, preferred_element_type=jnp.float32)
        gate, up, sig = swish(pre_ref[i], hidden)
        act = gate * sig
        dot = jnp.sum(act * up * back, axis=1, keepdims=True)
        found = jnp.where(lane == first + i, dot, found)
        grad_up = back * act
        grad_gate = back * up * sig * (1.0 + gate * (1.0 - sig))
        kept.append(jnp.concatenate([grad_gate, grad_up], axis=1).astype(jnp.bfloat16))
    dots[...] = found
    for i in range(STEP):
        gate_up = w_ref[i, 0 : 2 * hidden, :]
        rows = jnp.dot(kept[i], gate_up, preferred_element_type=jnp.float32)
        keep(first + i, slots, rows.astype(jnp.bfloat16))

    @pl.when(first + STEP == half)
    def _():
        combine(rank_ref, slots, out_ref)
        low_rows = SLOTS // 2

        def one(s, carry):
            part = dots[pl.ds(pl.multiple_of(s * SLOTS, SLOTS), SLOTS), 0:half]
            high = part.astype(jnp.bfloat16).astype(jnp.float32)
            low = part - high
            blank = jnp.zeros((low_rows, model - 4 * half), jnp.float32)
            line = [high[0:low_rows], low[0:low_rows], high[low_rows:], low[low_rows:], blank]
            out_ref[s, tok : tok + low_rows, :] = jnp.concatenate(line, axis=1).astype(jnp.bfloat16)
            return carry

        lax.fori_loop(0, sources, one, 0, unroll=4)


def params():
    return pltpu.CompilerParams(dimension_semantics=("arbitrary",), vmem_limit_bytes=VMEM)


def each(e):
    return (e, 0, 0)


def whole(e):
    return (0, 0, 0)


def gather_rows(ranks, rows):
    sources, half, tok = ranks.shape
    model = rows.shape[2]
    return pl.pallas_call(
        gather_kernel,
        grid=(sources,),
        in_specs=[
            pl.BlockSpec((1, half, tok), each),
            pl.BlockSpec((1, rows.shape[1], model), each),
        ],
        out_specs=pl.BlockSpec((half, SLOTS, model), lambda s: (0, s, 0)),
        out_shape=jax.ShapeDtypeStruct((half, sources * SLOTS, model), jnp.bfloat16),
        compiler_params=params(),
        cost_estimate=pl.CostEstimate(
            flops=2 * sources * half * SLOTS * tok * model,
            bytes_accessed=2 * half * sources * SLOTS * model + 2 * rows.size,
            transcendentals=0,
        ),
        name="gather_rows",
    )(ranks, rows)


def forward(weights, x_rows, scales, ranks):
    half, w_rows, model = weights.shape
    hidden = w_rows // 3
    sources, _, tok = ranks.shape
    rows = sources * SLOTS
    return pl.pallas_call(
        forward_kernel,
        grid=(half // STEP,),
        in_specs=[
            pl.BlockSpec((STEP, w_rows, model), each),
            pl.BlockSpec((STEP, rows, model), each),
            pl.BlockSpec((STEP, 8, rows), each),
            pl.BlockSpec((sources, half, tok), whole),
        ],
        out_specs=[
            pl.BlockSpec((sources, tok, model), whole),
            pl.BlockSpec((STEP, rows, 2 * hidden), each),
        ],
        out_shape=[
            jax.ShapeDtypeStruct((sources, tok, model), jnp.bfloat16),
            jax.ShapeDtypeStruct((half, rows, 2 * hidden), jnp.float32),
        ],
        scratch_shapes=[
            pltpu.VMEM((sources, half * SLOTS, model), jnp.bfloat16),
        ],
        compiler_params=params(),
        cost_estimate=pl.CostEstimate(
            flops=6 * half * rows * hidden * model,
            bytes_accessed=2 * (weights.size + x_rows.size),
            transcendentals=half * rows * hidden,
        ),
        name="forward_experts",
    )(weights, x_rows, scales, ranks)


def backward(weights, pre, scales, ranks, cotangents):
    half, w_rows, model = weights.shape
    sources, _, tok = ranks.shape
    rows = sources * SLOTS
    out_rows = tok + SLOTS // 2
    return pl.pallas_call(
        backward_kernel,
        grid=(half // STEP,),
        in_specs=[
            pl.BlockSpec((STEP, w_rows, model), each),
            pl.BlockSpec((STEP, rows, pre.shape[2]), each),
            pl.BlockSpec((sources, 8, half * SLOTS), whole),
            pl.BlockSpec((sources, half, tok), whole),
            pl.BlockSpec((sources, tok, model), whole),
        ],
        out_specs=pl.BlockSpec((sources, out_rows, model), whole),
        out_shape=jax.ShapeDtypeStruct((sources, out_rows, model), jnp.bfloat16),
        scratch_shapes=[
            pltpu.VMEM((sources, half * SLOTS, model), jnp.bfloat16),
            pltpu.VMEM((rows, 128), jnp.float32),
        ],
        compiler_params=params(),
        cost_estimate=pl.CostEstimate(
            flops=60 * half * rows * (w_rows // 3) * model,
            bytes_accessed=2 * (weights.size + 2 * pre.size),
            transcendentals=half * rows * (w_rows // 3),
        ),
        name="backward_experts",
    )(weights, pre, scales, ranks, cotangents)


def body(tokens, expert_ids, router_gates, w_in, w_down, cotangent):
    tok, model = tokens.shape
    planes = lax.axis_size("dp")
    side = 4
    half = lax.axis_size("expert")
    experts = 2 * half
    parity = lax.rem(lax.axis_index("dp") // side, 2)

    def both_slices(which):
        pair = lax.dynamic_index_in_dim(w_in, which, 0, keepdims=False)
        down = lax.dynamic_slice_in_dim(w_down, which, 1, 0)
        return jnp.concatenate([pair, down], axis=0)

    swap = [(d, (((d // side) ^ 1) * side) + d % side) for d in range(planes)]
    other = lax.ppermute(both_slices(1 - parity), "dp", swap)
    mine = jnp.concatenate([both_slices(parity), other], axis=1).reshape(-1, model)
    weights = lax.all_gather(mine, "expert", axis=0, tiled=False)

    ids = expert_ids.T
    match = ids[:, None, :] == jnp.arange(experts, dtype=jnp.int32)[None, :, None]
    chosen = jnp.any(match, axis=0)
    gate_of = jnp.sum(jnp.where(match, router_gates.T[:, None, :], 0.0), axis=0)
    earlier = jnp.arange(tok)[:, None] < jnp.arange(tok)[None, :]
    rank = jnp.dot(
        chosen.astype(jnp.bfloat16), earlier.astype(jnp.bfloat16), preferred_element_type=jnp.float32
    )
    rank = jnp.where(chosen, rank, -1.0)
    slot_no = jnp.arange(SLOTS, dtype=jnp.float32)
    at_slot = rank[:, None, :] == slot_no[None, :, None]
    slot_gate = jnp.sum(jnp.where(at_slot, gate_of[:, None, :], 0.0), axis=2)
    gate_high = lax.reduce_precision(slot_gate, 8, 7)
    gate_low = slot_gate - gate_high

    def facts(odd):
        flat = lambda a: a.reshape(half, 2, -1)[:, odd].reshape(-1)
        return jnp.concatenate([flat(rank), flat(gate_high), flat(gate_low)]).astype(jnp.bfloat16)

    fact_rows = 8
    known = jnp.stack([facts(0), facts(1)])
    known = jnp.pad(known, ((0, 0), (0, fact_rows * model - known.shape[1])))
    known = known.reshape(2, 1, fact_rows, model)
    known = jnp.broadcast_to(known[:, None], (2, side, 1, fact_rows, model)).reshape(
        1, 2 * side, fact_rows, model
    )
    known = jnp.broadcast_to(known, (planes // (2 * side), 2 * side, fact_rows, model))
    known = known.reshape(planes, fact_rows, model)
    spread = lambda a: jnp.broadcast_to(a[None], (planes, tok, model))
    swap_rows = lambda a: lax.all_to_all(a, "dp", split_axis=0, concat_axis=0, tiled=True)
    rows = swap_rows(jnp.concatenate([spread(tokens), known], axis=1))
    cotangents = swap_rows(spread(cotangent))

    facts_in = rows[:, tok:, :].reshape(planes, fact_rows * model).astype(jnp.float32)
    first, second = half * tok, half * tok + half * SLOTS
    ranks = facts_in[:, 0:first].reshape(planes, half, tok)
    scales = facts_in[:, first:second] + facts_in[:, second : second + half * SLOTS]
    by_source = jnp.broadcast_to(scales[:, None], (planes, 8, half * SLOTS))
    scales = scales.reshape(planes, half, SLOTS).swapaxes(0, 1).reshape(half, 1, planes * SLOTS)
    scales = jnp.broadcast_to(scales, (half, 8, planes * SLOTS))

    x_rows = gather_rows(ranks, rows)
    layer_part, pre = forward(weights, x_rows, scales, ranks)
    along_x = [[x * side + y for x in range(planes // side)] for y in range(side)]
    along_y = [[x * side + y for y in range(side)] for x in range(planes // side)]
    grad_part = backward(weights, pre, by_source, ranks, cotangents)
    layer_output = layer_part.reshape(planes * tok, model)
    for groups in (along_x, along_y):
        layer_output = lax.psum_scatter(
            layer_output, "dp", scatter_dimension=0, axis_index_groups=groups, tiled=True
        )
    grad_in = swap_rows(grad_part).astype(jnp.float32)
    token_grads = jnp.sum(grad_in[:, 0:tok], axis=0).astype(jnp.bfloat16)

    dots = grad_in[:, tok:, 0 : 4 * half].reshape(2, 2, side, SLOTS // 2, 2, 2, half)
    dots = jnp.sum(dots, axis=(0, 2, 5))
    dots = dots.transpose(3, 0, 2, 1).reshape(experts, SLOTS)
    by_expert = jnp.sum(jnp.where(at_slot, dots[:, :, None], 0.0), axis=1)
    gate_grads = jnp.sum(jnp.where(match, by_expert[None], 0.0), axis=1).T / router_gates
    return (layer_output, token_grads, gate_grads)


def solution(mesh):
    both = P(("dp", "expert"), None)
    placed = (both, both, both, P("expert", None, "dp", None), P("expert", "dp", None), both)
    return jax.shard_map(
        body, mesh=mesh, in_specs=placed, out_specs=(both, both, both), check_vma=False
    )
```
